128 devices in a mesh: grp: 8 (over z_hi, x), sub: 16 (over z_lo, y, core).
Axes of the slice: x: 4, y: 4, z: 4 (z_hi: 2, z_lo: 2; z = z_hi * 2 + z_lo), core: 2. Of those that a mesh axis runs over, the one named last changes fastest.
Arguments:
- residual_field: float32 [16, 32, 128, 384], P('grp', 'sub'), may hold values from -6 to 6
- line_inverse: bfloat16 [32, 64, 5, 384, 384], P('grp', 'sub'), may hold values from -5 to 5
- deflation: bfloat16 [16, 32, 48, 384], P('grp', 'sub'), may hold values from -0.21875 to 0.21875
- counts: int32 [8, 16], P('grp', 'sub'), may hold values from 12 to 48
- coarse_factor: float32 [6144, 6144], P(('grp', 'sub')), may hold values from -2 to 2, as said below
Outputs:
- preconditioned: float32 [16, 32, 128, 384], P('grp', 'sub')
The draws below stay inside these ranges and needn't reach their ends.
Inputs may be any that keep to these rules, and one draw needn't show every extreme that they name: `coarse_factor`: lower triangular with a positive diagonal.
All inputs are finite; a program needn't handle non-finite values.
Results may differ from the reference program's by a relative error of at most 0.0029.
Values may be sent and summed in bfloat16 or wider, within the bound.
No kernel may reach another device: no remote copies, remote signals or barrier semaphores. Data moves between devices by JAX's collectives and lax.ppermute only.
A program may use at most 128 MiB of HBM per device.

```python
import math
import jax
import jax.numpy as jnp
from jax import lax

CX = 2
CY = 2
RHS = 128
SLOTS = 48
LINE = 384
NX = 16
NY = 32
NCOARSE = 6144
N_GRP = 8
N_SUB = 16


def draw_line_inverse(key, part):
    key = jax.random.fold_in(key, 11)
    noise_key, scale_key = jax.random.split(key)
    shape = (N_GRP * (CX + 2), N_SUB * (CY + 2), 5, LINE, LINE)
    noise = jnp.clip(jax.random.normal(noise_key, shape, jnp.float32), -4.0, 4.0)
    stiffness = jnp.exp(jax.random.uniform(scale_key, (shape[0], shape[1], 1, 1, LINE), jnp.float32, math.log(0.3), math.log(3.0)))
    row_ids = lax.broadcasted_iota(jnp.int32, (1, 1, 5, LINE, LINE), 3)
    col_ids = lax.broadcasted_iota(jnp.int32, (1, 1, 5, LINE, LINE), 4)
    block_ids = lax.broadcasted_iota(jnp.int32, (1, 1, 5, LINE, LINE), 2)
    centre = (block_ids == 2).astype(jnp.float32)
    diagonal_part = centre * (row_ids == col_ids).astype(jnp.float32)
    spread = (0.6 * centre + 0.3 * (1.0 - centre)) / math.sqrt(LINE)
    return ((noise * spread + diagonal_part) * stiffness).astype(jnp.bfloat16)


def draw_coarse_factor(key, part):
    key = jax.random.fold_in(key, 23)
    noise_key, diag_key = jax.random.split(key)
    shape = (NCOARSE, NCOARSE)
    row_ids = lax.broadcasted_iota(jnp.int32, shape, 0)
    col_ids = lax.broadcasted_iota(jnp.int32, shape, 1)
    below = jnp.clip(jax.random.normal(noise_key, shape, jnp.float32), -4.0, 4.0)
    below = below * 0.6 / jnp.sqrt(row_ids.astype(jnp.float32) + 1.0)
    diagonal_vals = jnp.exp(jax.random.uniform(diag_key, shape, jnp.float32, math.log(0.5), math.log(1.5)))
    upper_part = jnp.where(row_ids == col_ids, diagonal_vals, jnp.zeros(shape, jnp.float32))
    return jnp.where(col_ids < row_ids, below, upper_part)


def draw_counts(key, part):
    key = jax.random.fold_in(key, 37)
    first_key, second_key, third_key = jax.random.split(key, 3)
    total_domains = N_GRP * N_SUB
    drawn = jax.random.randint(first_key, (total_domains,), SLOTS // 4, SLOTS + 1)
    top_at = jax.random.randint(second_key, (), 0, total_domains)
    low_at = (top_at + 1 + jax.random.randint(third_key, (), 0, total_domains - 1)) % total_domains
    domain_ids = jnp.arange(total_domains, dtype=jnp.int32)
    drawn = jnp.where(domain_ids == top_at, SLOTS, drawn)
    drawn = jnp.where(domain_ids == low_at, SLOTS // 4, drawn)
    return drawn.reshape(N_GRP, N_SUB).astype(jnp.int32)


def levels(rng, dims, cuts, low, high):
    factor_of = 1.0
    for axis_at, shards_of in cuts:
        steps = jax.random.uniform(jax.random.fold_in(jax.random.fold_in(rng, 6), axis_at), (shards_of,), jnp.float32, low / len(cuts), high / len(cuts))
        factor_of = factor_of * jnp.repeat(jnp.exp(steps), dims[axis_at] // shards_of).reshape((-1,) + (1,) * (len(dims) - 1 - axis_at))
    return factor_of


def scatter_about(own_key, dims, deviation, reach, cuts=(), kind=jnp.bfloat16):
    loudness = levels(own_key, dims, cuts, -0.22, 0.18) if cuts else 1.0
    array = jax.random.normal(own_key, dims, jnp.float32) * deviation * loudness
    return jnp.minimum(jnp.maximum(array, -reach), reach).astype(kind)


def setup_inputs(seed: int = 0) -> dict:
    key_of = jax.random.split(jax.random.key(seed), 6)
    return {
        "residual_field": scatter_about(key_of[0], (NX, NY, RHS, LINE), 1.0, 6.0, ((0, 8), (1, 16)), jnp.float32),
        "line_inverse": draw_line_inverse(jax.random.fold_in(key_of[5], 71), 0),
        "deflation": scatter_about(key_of[2], (NX, NY, SLOTS, LINE), (CX * CY * LINE // 2) ** -0.5, 0.21875, ((0, 8), (1, 16))),
        "counts": draw_counts(jax.random.fold_in(key_of[5], 71), 0),
        "coarse_factor": draw_coarse_factor(jax.random.fold_in(key_of[5], 71), 0),
    }


NEIGHBOUR_STEPS = ((-1, 0), (0, -1), (0, 0), (0, 1), (1, 0))


def reference(residual_field, line_inverse, deflation, counts, coarse_factor):
    rounded = residual_field.astype(jnp.bfloat16)
    wide_x = CX + 2
    wide_y = CY + 2
    padded = jnp.pad(rounded, ((2, 2), (2, 2), (0, 0), (0, 0)))
    accumulated = jnp.zeros((NX + 2, NY + 2, RHS, LINE), jnp.float32)

    def one_domain(running, domain):
        grp_at = (domain // N_SUB).astype(jnp.int32)
        sub_at = (domain % N_SUB).astype(jnp.int32)
        anchor = jnp.int32(0)
        corner = (grp_at * CX, sub_at * CY, anchor, anchor)
        window = lax.dynamic_slice(padded, (grp_at * CX + 1, sub_at * CY + 1, anchor, anchor), (wide_x, wide_y, RHS, LINE))
        framed = jnp.pad(window, ((1, 1), (1, 1), (0, 0), (0, 0))).astype(jnp.float32)
        blocks = lax.dynamic_slice(line_inverse, (grp_at * wide_x, sub_at * wide_y, anchor, anchor, anchor), (wide_x, wide_y, 5, LINE, LINE))
        local_sol = jnp.zeros((wide_x, wide_y, RHS, LINE), jnp.float32)
        for index, (step_p, step_q) in enumerate(NEIGHBOUR_STEPS):
            shifted = framed[1 + step_p:1 + step_p + wide_x, 1 + step_q:1 + step_q + wide_y]
            local_sol = local_sol + jnp.einsum('abru,abuv->abrv', shifted, blocks[:, :, index].astype(jnp.float32))
        current = lax.dynamic_slice(running, corner, (wide_x, wide_y, RHS, LINE))
        return lax.dynamic_update_slice(running, current + local_sol, corner), None

    accumulated, unused = lax.scan(one_domain, accumulated, jnp.arange(N_GRP * N_SUB, dtype=jnp.int32))
    schwarz = accumulated[1:-1, 1:-1]
    shaped_z = deflation.reshape(N_GRP, CX, N_SUB, CY, SLOTS, LINE).astype(jnp.float32)
    shaped_r = rounded.reshape(N_GRP, CX, N_SUB, CY, RHS, LINE).astype(jnp.float32)
    coarse_in = jnp.einsum('gasbku,gasbru->gskr', shaped_z, shaped_r)
    slot_ids = jnp.arange(SLOTS, dtype=jnp.int32)
    keeper = (slot_ids[None, None, :] < counts[:, :, None]).astype(jnp.float32)
    coarse_in = (coarse_in * keeper[..., None]).reshape(NCOARSE, RHS)
    lowered = jnp.dot(coarse_factor, coarse_in, precision=lax.Precision.HIGHEST)
    solved = jnp.dot(coarse_factor.T, lowered, precision=lax.Precision.HIGHEST)
    solved = (solved.reshape(N_GRP, N_SUB, SLOTS, RHS) * keeper[..., None]).astype(jnp.bfloat16)
    correction = jnp.einsum('gasbku,gskr->gasbru', shaped_z, solved.astype(jnp.float32))
    return schwarz + correction.reshape(NX, NY, RHS, LINE)
```

```python
import jax
import jax.numpy as jnp
from jax import lax
from jax.experimental import pallas as pl
from jax.experimental.pallas import tpu as pltpu
from jax.sharding import Mesh, PartitionSpec as P

AXES = ("zh", "x", "zl", "y", "c")
GRP = ("zh", "x")
SUB = ("zl", "y", "c")
RING = ("zh", "zl")
GATHER = ("x", "y", "c")

STEPS = ((-1, 0), (0, -1), (0, 0), (0, 1), (1, 0))
WIDE = 4


def shift(value, axes, size, step):
    pairs = [(i, i + step) for i in range(size) if 0 <= i + step < size]
    return lax.ppermute(value, axes, pairs)


def rotate(value, axes, size, step):
    return lax.ppermute(value, axes, [(i, (i + step) % size) for i in range(size)])


def terms(a, b):
    found = []
    for k, (p, q) in enumerate(STEPS):
        if 0 <= a + p < WIDE and 0 <= b + q < WIDE:
            found.append((k, a + p, b + q))
    return found


def line_kernel(cells, own, low_x, high_x, low_y, high_y, blocks, *rest):
    outs, (held, sems) = rest[:-2], rest[-2:]

    def window(a, b):
        if b == 0:
            return low_y[a, 0]
        if b == WIDE - 1:
            return high_y[a, 0]
        if a == 0:
            return low_x[0, b - 1]
        if a == WIDE - 1:
            return high_x[0, b - 1]
        return own[a - 1, b - 1]

    slot = 0
    plan = []
    for a, b, _, _ in cells:
        mine = []
        for k, sa, sb in terms(a, b):
            copy = pltpu.make_async_copy(blocks.at[a, b, k], held.at[slot], sems.at[slot])
            copy.start()
            mine.append((copy, slot, sa, sb))
            slot += 1
        plan.append(mine)
    for (a, b, out, at), mine in zip(cells, plan):
        total = None
        for copy, place, sa, sb in mine:
            copy.wait()
            part = jnp.dot(window(sa, sb), held[place], preferred_element_type=jnp.float32)
            total = part if total is None else total + part
        outs[out][at] = total.astype(outs[out].dtype)


def line_solve(cells, shapes, windows, line_inverse):
    count = sum(len(terms(a, b)) for a, b, _, _ in cells)
    line = line_inverse.shape[-1]
    rhs = windows[0].shape[2]

    def body(*refs):
        line_kernel(cells, *refs)

    return pl.pallas_call(
        body,
        out_shape=[jax.ShapeDtypeStruct(s, d) for s, d in shapes],
        in_specs=[pl.BlockSpec(memory_space=pltpu.VMEM)] * 5 + [pl.BlockSpec(memory_space=pl.ANY)],
        out_specs=[pl.BlockSpec(memory_space=pltpu.VMEM)] * len(shapes),
        scratch_shapes=[
            pltpu.VMEM((count, line, line), line_inverse.dtype),
            pltpu.SemaphoreType.DMA((count,)),
        ],
        compiler_params=pltpu.CompilerParams(vmem_limit_bytes=40 * 1024 * 1024),
        cost_estimate=pl.CostEstimate(
            flops=2 * count * rhs * line * line, bytes_accessed=count * line * line * 2, transcendentals=0
        ),
    )(*windows, line_inverse)


def schwarz_solve(rounded, line_inverse, n_grp, n_sub):
    rhs, line = rounded.shape[2:]
    low_x = shift(rounded[1:2], GRP, n_grp, 1)
    high_x = shift(rounded[0:1], GRP, n_grp, -1)
    low_y = shift(jnp.concatenate([low_x[:, 1:2], rounded[:, 1:2], high_x[:, 1:2]], 0), SUB, n_sub, 1)
    high_y = shift(jnp.concatenate([low_x[:, 0:1], rounded[:, 0:1], high_x[:, 0:1]], 0), SUB, n_sub, -1)
    windows = (rounded, low_x, high_x, low_y, high_y)

    edge = ((WIDE, 1, rhs, line), jnp.bfloat16)
    cells = [(a, b, i, (a, 0)) for a in range(WIDE) for i, b in enumerate((0, WIDE - 1))]
    to_low, to_high = line_solve(cells, [edge, edge], windows, line_inverse)
    back_low = shift(to_high, SUB, n_sub, 1)
    back_high = shift(to_low, SUB, n_sub, -1)

    whole = ((WIDE, 2, rhs, line), jnp.float32)
    cells = [(a, b, 0, (a, b - 1)) for a in (0, WIDE - 1, 1, 2) for b in (1, 2)]
    (middle,) = line_solve(cells, [whole], windows, line_inverse)
    folded = middle + jnp.concatenate([back_low, back_high], 1).astype(jnp.float32)

    from_low = shift(folded[3:4].astype(jnp.bfloat16), GRP, n_grp, 1)
    from_high = shift(folded[0:1].astype(jnp.bfloat16), GRP, n_grp, -1)
    return folded[1:3] + jnp.concatenate([from_low, from_high], 0).astype(jnp.float32)


def coarse_solve(rounded, deflation, counts, coarse_factor, sizes):
    slots = deflation.shape[2]
    rhs = rounded.shape[2]
    ring = sizes["zh"] * sizes["zl"]
    group = sizes["x"] * sizes["y"] * sizes["c"]
    keeper = (lax.broadcasted_iota(jnp.int32, (slots, 1), 0) < counts).astype(jnp.float32)

    parts = coarse_factor.reshape(slots, sizes["zh"], sizes["x"], sizes["zl"], -1)
    here = lax.axis_index(RING)
    rows = []
    for step in range(ring):
        there = lax.rem(here + step, ring)
        block = lax.dynamic_slice(
            parts,
            (0, there // sizes["zl"], 0, lax.rem(there, sizes["zl"]), 0),
            (slots, 1, sizes["x"], 1, parts.shape[-1]),
        ).reshape(slots, -1)
        rows.append(rotate(block, RING, ring, step) if step else block)
    factor = jnp.concatenate(rows, 0)

    coarse_part = jnp.einsum("abku,abru->kr", deflation, rounded, preferred_element_type=jnp.float32) * keeper
    spread = jnp.broadcast_to(coarse_part[None], (group, slots, rhs))
    gathered = lax.all_to_all(spread, GATHER, 0, 0).reshape(group * slots, rhs)

    partial = jnp.dot(factor, gathered, precision=lax.Precision.HIGHEST, preferred_element_type=jnp.float32)
    lowered = partial.reshape(ring, slots, rhs)
    total = lowered
    for step in range(1, ring):
        total = total + jnp.roll(rotate(lowered, RING, ring, step), step, 0)
    terms_back = jnp.dot(
        factor.T, total.reshape(ring * slots, rhs), precision=lax.Precision.HIGHEST, preferred_element_type=jnp.float32
    )
    solved = lax.all_to_all(terms_back.reshape(group, slots, rhs), GATHER, 0, 0).sum(0)
    solved = (solved * keeper).astype(jnp.bfloat16)
    return jnp.einsum("abku,kr->abru", deflation, solved, preferred_element_type=jnp.float32)


def solution(mesh):
    n_grp, n_sub = mesh.shape["grp"], mesh.shape["sub"]
    sizes = {"zh": 2, "x": n_grp // 2, "zl": 2, "y": n_sub // 4, "c": 2}
    fine = Mesh(mesh.devices.reshape([sizes[a] for a in AXES]), AXES)

    def body(residual_field, line_inverse, deflation, counts, coarse_factor):
        rounded = residual_field.astype(jnp.bfloat16)
        schwarz = schwarz_solve(rounded, line_inverse, n_grp, n_sub)
        return schwarz + coarse_solve(rounded, deflation, counts, coarse_factor, sizes)

    return jax.shard_map(
        body,
        mesh=fine,
        in_specs=(
            P(GRP, SUB, None, None),
            P(GRP, SUB, None, None, None),
            P(GRP, SUB, None, None),
            P(GRP, SUB),
            P(AXES, None),
        ),
        out_specs=P(GRP, SUB, None, None),
        check_vma=False,
    )
```

```python
import jax
import jax.numpy as jnp
from jax import lax
from jax.experimental import pallas as pl
from jax.experimental.pallas import tpu as pltpu
from jax.sharding import Mesh, PartitionSpec as P

AXES = ("zh", "x", "zl", "y", "c")
GRP = ("zh", "x")
SUB = ("zl", "y", "c")
SPREAD = ("zh", "x", "y")

STEPS = ((-1, 0), (0, -1), (0, 0), (0, 1), (1, 0))
WIDE = 4
VMEM = pl.BlockSpec(memory_space=pltpu.VMEM)
SMEM = pl.BlockSpec(memory_space=pltpu.SMEM)
ANY = pl.BlockSpec(memory_space=pl.ANY)
HBM = pl.BlockSpec(memory_space=pltpu.HBM)
MIB = 1024 * 1024
F32 = jnp.float32
BF16 = jnp.bfloat16


def limit(mib):
    return pltpu.CompilerParams(vmem_limit_bytes=mib * MIB)


def struct(shape, dtype):
    return jax.ShapeDtypeStruct(shape, dtype)


def estimate(flops, size):
    return pl.CostEstimate(flops=flops, bytes_accessed=size, transcendentals=0)


def swap(value, axis):
    return lax.ppermute(value, axis, [(0, 1), (1, 0)])


def swap_across(value):
    return lax.ppermute(value, ("zl", "c"), [(i, 3 - i) for i in range(4)])


def swap_pairs(value, axes, size, begin):
    pairs = []
    for i in range(begin, size - 1, 2):
        pairs += [(i, i + 1), (i + 1, i)]
    return lax.ppermute(value, axes, pairs)


def swap_outward(value, size):
    pairs = []
    for i in range(1, size, 2):
        pairs += [(i, (i + 1) % size), ((i + 1) % size, i)]
    return lax.ppermute(value, SUB, pairs)


def present(flag, value):
    return jnp.where(flag, value, jnp.zeros_like(value))


def terms(a, b):
    found = []
    for k, (p, q) in enumerate(STEPS):
        if 0 <= a + p < WIDE and 0 <= b + q < WIDE:
            found.append((k, a + p, b + q))
    return found


def position():
    spot = {axis: lax.axis_index(axis) for axis in AXES}
    size = {axis: lax.axis_size(axis) for axis in AXES}
    core, x = spot["c"], spot["x"]
    before = jnp.logical_or(spot["zh"] > 0, x > 0)
    after = jnp.logical_or(spot["zh"] < size["zh"] - 1, x < size["x"] - 1)
    outward = spot["zl"] * size["y"] + spot["y"]
    past = jnp.where(core == 0, outward > 0, outward < size["zl"] * size["y"] - 1)
    return core, before, after, past, lax.rem(x, 2)


def line_kernel(cells, put, own, ends, pair, outer, blocks, *rest):
    at = position()
    more, (sides, held, sems) = rest[:-3], rest[-3:]
    slot, plan = 0, []
    for a, b in cells:
        found = terms(a, b)
        start, run, copies = slot, 0, []
        for i, (k, _, _) in enumerate(found):
            run += 1
            if i + 1 == len(found) or found[i + 1][0] != k + 1:
                source = blocks.at[a, b, pl.ds(k + 1 - run, run)]
                copies.append(pltpu.make_async_copy(source, held.at[pl.ds(slot, run)], sems.at[slot]))
                copies[-1].start()
                slot, run = slot + run, 0
        plan.append((start, copies, found))

    first = at[0] == 0
    for a in range(WIDE):
        near, far = pair[a, 0], present(at[3], outer[a, 0])
        sides[0, a] = jnp.where(first, far, near)
        sides[1, a] = jnp.where(first, near, far)

    def window(a, b):
        if b == 0:
            return sides[0, a]
        if b == WIDE - 1:
            return sides[1, a]
        if a in (0, WIDE - 1):
            return ends[0 if a == 0 else 1, b - 1]
        return own[a - 1, b - 1]

    line = held.shape[-1]
    for (a, b), (start, copies, found) in zip(cells, plan):
        for copy in copies:
            copy.wait()
        sources = jnp.concatenate([window(sa, sb) for _, sa, sb in found], axis=1)
        weights = held[start : start + len(found)].reshape(len(found) * line, line)
        put(a, b, jnp.dot(sources, weights, preferred_element_type=F32), at, more)


def line_solve(cells, put, shapes, windows, line_inverse, extra=()):
    count = sum(len(terms(a, b)) for a, b in cells)
    line = line_inverse.shape[-1]
    rhs = windows[0].shape[2]

    def body(*refs):
        line_kernel(cells, put, *refs)

    return pl.pallas_call(
        body,
        out_shape=shapes,
        in_specs=[VMEM] * 4 + [HBM] + [VMEM] * len(extra),
        out_specs=[VMEM] * len(shapes),
        scratch_shapes=[
            pltpu.VMEM((2, WIDE, rhs, line), BF16),
            pltpu.VMEM((count, line, line), line_inverse.dtype),
            pltpu.SemaphoreType.DMA((count,)),
        ],
        compiler_params=limit(42),
        cost_estimate=estimate(2 * count * rhs * line * line, count * line * line * 2),
    )(*windows, line_inverse, *extra)


def put_rim(a, b, value, at, refs):
    value = value.astype(BF16)
    first = at[0] == 0
    to_pair = first if b else jnp.logical_not(first)

    @pl.when(to_pair)
    def _():
        refs[0][a, 0] = value

    @pl.when(jnp.logical_not(to_pair))
    def _():
        refs[1][a, 0] = value


def returned(at, from_pair, from_outer, a, b):
    near, far = from_pair[a, 0], present(at[3], from_outer[a, 0])
    return jnp.where((at[0] == 0) == (b == 1), far, near).astype(F32)


def put_rows(a, b, value, at, refs):
    from_pair, from_outer, near, far = refs
    value = (value + returned(at, from_pair, from_outer, a, b)).astype(BF16)
    to_near = (at[4] == 0) == (a != 0)

    @pl.when(to_near)
    def _():
        near[0, b - 1] = value

    @pl.when(jnp.logical_not(to_near))
    def _():
        far[0, b - 1] = value


def put_inner(a, b, value, at, refs):
    refs[-1][a - 1, b - 1] = value


def columns(near, far, rounded):
    rhs, line = rounded.shape[2:]

    def body(near, far, rounded, pair, outer, own, ends):
        at = position()
        first, even = at[0] == 0, at[4] == 0
        for a in range(WIDE):
            if a in (0, WIDE - 1):
                for b in range(2):
                    low, high = (far, near) if a == 0 else (near, far)
                    ends[a // 2, b] = present(at[1 + a // 2], jnp.where(even, low[0, b], high[0, b]))
                left, right = ends[a // 2, 0], ends[a // 2, 1]
            else:
                left, right = rounded[a - 1, 0], rounded[a - 1, 1]
                own[a - 1, 0], own[a - 1, 1] = left, right
            pair[a, 0] = jnp.where(first, right, left)
            outer[a, 0] = jnp.where(first, left, right)

    out, square = struct((WIDE, 1, rhs, line), BF16), struct(rounded.shape, BF16)
    return pl.pallas_call(
        body,
        out_shape=[out, out, square, square],
        in_specs=[VMEM] * 3,
        out_specs=[VMEM] * 4,
        compiler_params=limit(4),
    )(near, far, rounded)


def rim_lines(windows, line_inverse):
    _, _, rhs, line = windows[0].shape
    column = struct((WIDE, 1, rhs, line), BF16)
    cells = [(a, b) for a in range(WIDE) for b in (0, WIDE - 1)]
    return line_solve(cells, put_rim, [column, column], windows, line_inverse)


def row_lines(windows, line_inverse, from_pair, from_outer):
    _, _, rhs, line = windows[0].shape
    row = struct((1, 2, rhs, line), BF16)
    cells = [(a, b) for a in (0, WIDE - 1) for b in (1, 2)]
    return line_solve(cells, put_rows, [row, row], windows, line_inverse, (from_pair, from_outer))


def inner_lines(windows, line_inverse):
    cells = [(a, b) for a in (1, 2) for b in (1, 2)]
    return line_solve(cells, put_inner, [struct(windows[0].shape, F32)], windows, line_inverse)[0]


def collect(inner, from_pair, from_outer, from_near, from_far):
    cx, cy, _, _ = inner.shape

    def body(inner, from_pair, from_outer, from_near, from_far, out):
        at = position()
        for a in range(cx):
            for b in range(cy):
                side = returned(at, from_pair, from_outer, a + 1, b + 1)
                low, high = (from_far, from_near) if a == 0 else (from_near, from_far)
                across = present(at[1 + a], jnp.where(at[4] == 0, low[0, b], high[0, b])).astype(F32)
                out[a, b] = inner[a, b] + side + across

    return pl.pallas_call(
        body,
        out_shape=struct(inner.shape, F32),
        in_specs=[VMEM] * 5,
        out_specs=VMEM,
        compiler_params=limit(8),
        cost_estimate=estimate(10**9, 4 * 10**6),
    )(inner, from_pair, from_outer, from_near, from_far)


def keep_mask(count, slots, rhs):
    return lax.broadcasted_iota(jnp.int32, (slots, rhs), 0) < count[0, 0]


def enter(residual_field, deflation, counts, copies):
    slots, line = deflation.shape[2:]
    cx, cy, rhs, _ = residual_field.shape

    def body(count, residual, vectors, rounded, near, far, spread, held, basis, cells, sums, sems):
        copies_in = []
        for a in range(cx):
            for b in range(cy):
                for n, (source, place) in enumerate(((residual, held), (vectors, basis))):
                    copy = pltpu.make_async_copy(source.at[a, b], place.at[a, b], sems.at[n, a, b])
                    copy.start()
                    copies_in.append(copy)
        total, copies_out = None, []
        for a in range(cx):
            for b in range(cy):
                for n in range(2):
                    copies_in[2 * (a * cy + b) + n].wait()
                value = held[a, b].astype(BF16)
                cells[a, b] = value
                part = lax.dot_general(
                    basis[a, b], value, (((1,), (1,)), ((), ())), preferred_element_type=F32
                )
                total = part if total is None else total + part
                copy = pltpu.make_async_copy(cells.at[a, b], rounded.at[a, b], sems.at[2, a, b])
                copy.start()
                copies_out.append(copy)
        even = position()[4] == 0
        for n, out in enumerate((near, far)):
            row = jnp.where(even, 1 - n, n)
            copy = pltpu.make_async_copy(cells.at[pl.ds(row, 1)], out, sems.at[3, n, 0])
            copy.start()
            copies_out.append(copy)
        total = jnp.where(keep_mask(count, slots, rhs), total, 0.0).astype(BF16)
        for i in range(copies):
            sums[i] = total
        copy = pltpu.make_async_copy(sums, spread, sems.at[0, 0, 0])
        copy.start()
        copy.wait()
        for copy in copies_out:
            copy.wait()

    row = struct((1, cy, rhs, line), BF16)
    return pl.pallas_call(
        body,
        out_shape=[struct(residual_field.shape, BF16), row, row, struct((copies, slots, rhs), BF16)],
        in_specs=[SMEM, HBM, HBM],
        out_specs=[HBM] * 4,
        scratch_shapes=[
            pltpu.VMEM(residual_field.shape, F32),
            pltpu.VMEM(deflation.shape, deflation.dtype),
            pltpu.VMEM(residual_field.shape, BF16),
            pltpu.VMEM((copies, slots, rhs), BF16),
            pltpu.SemaphoreType.DMA((4, cx, cy)),
        ],
        compiler_params=limit(60),
    )(counts, residual_field, deflation)


def halves(value):
    high = value.astype(BF16)
    return high, (value - high.astype(F32)).astype(BF16)


def cut_factor(factor, blocks, width):
    slots = factor.shape[0]

    def body(factor, *refs):
        outs, (held, sems, out_sems) = refs[:2], refs[2:]
        half = lax.axis_index("zl")
        copies = []
        for n, side in ((1, 1 - half), (0, half)):
            for j in range(blocks):
                start = pl.multiple_of((2 * j + side) * width, width)
                copy = pltpu.make_async_copy(factor.at[:, pl.ds(start, width)], held.at[n, j], sems.at[n, j])
                copy.start()
                copies.append(copy)
        saves = []
        for n in (1, 0):
            for j in range(blocks):
                copies[(1 - n) * blocks + j].wait()
            saves.append(pltpu.make_async_copy(held.at[n], outs[n], out_sems.at[n]))
            saves[-1].start()
        for save in saves:
            save.wait()

    return pl.pallas_call(
        body,
        out_shape=[struct((blocks, slots, width), F32)] * 2,
        in_specs=[HBM],
        out_specs=[HBM] * 2,
        scratch_shapes=[
            pltpu.VMEM((2, blocks, slots, width), F32),
            pltpu.SemaphoreType.DMA((2, blocks)),
            pltpu.SemaphoreType.DMA((2,)),
        ],
        compiler_params=limit(60),
    )(factor)


def lower(rows, gathered):
    blocks, slots, width = rows[0].shape
    count, _, rhs = gathered.shape
    per = count // blocks
    sets = len(rows)

    def body(*refs):
        rows, (gathered, out) = refs[:sets], refs[sets:]
        first = lax.axis_index("c") == 0
        zero = jnp.zeros((slots, rhs), BF16)
        total = None
        for j in range(blocks):
            pieces = []
            for y in range(per):
                mine = gathered[j * per + y]
                pieces += [jnp.where(first, mine, zero), jnp.where(first, zero, mine)]
            high, low = halves(jnp.concatenate([r[j] for r in rows], 0))
            part = jnp.dot(
                jnp.concatenate([high, low], 0), jnp.concatenate(pieces, 0), preferred_element_type=F32
            )
            total = part if total is None else total + part
        for n in range(sets):
            out[n] = total[n * slots : (n + 1) * slots] + total[(sets + n) * slots : (sets + n + 1) * slots]

    return pl.pallas_call(
        body,
        out_shape=struct((sets, slots, rhs), F32),
        in_specs=[VMEM] * (sets + 1),
        out_specs=VMEM,
        compiler_params=limit(8),
    )(*rows, gathered)


def raise_back(rows, partials):
    blocks, slots, width = rows[0].shape
    rhs = partials[0].shape[2]
    per = width // (2 * slots)
    sets = len(rows)

    def body(*refs):
        rows, partials, (out, made, sems) = refs[:sets], refs[sets : 2 * sets], refs[2 * sets :]
        first = lax.axis_index("c") == 0
        sums = []
        for n in range(sets):
            total = partials[0][n]
            for m in range(1, sets):
                total = total + partials[m][n ^ m]
            sums.append(total)
        lowered_high, lowered_low = halves(jnp.concatenate(sums, 0))
        over = (((0,), (0,)), ((), ()))
        copies = []
        for j in range(blocks):
            high, low = halves(jnp.concatenate([r[j] for r in rows], 0))
            part = lax.dot_general(high, lowered_high, over, preferred_element_type=F32)
            part = part + lax.dot_general(high, lowered_low, over, preferred_element_type=F32)
            part = part + lax.dot_general(low, lowered_high, over, preferred_element_type=F32)
            for y in range(per):
                a = part[2 * y * slots : (2 * y + 1) * slots]
                b = part[(2 * y + 1) * slots : (2 * y + 2) * slots]
                made[j * per + y] = jnp.where(first, a, b).astype(BF16)
            piece = pl.ds(j * per, per)
            copies.append(pltpu.make_async_copy(made.at[piece], out.at[piece], sems.at[j]))
            copies[j].start()
        for copy in copies:
            copy.wait()

    shape = (blocks * per, slots, rhs)
    return pl.pallas_call(
        body,
        out_shape=struct(shape, BF16),
        in_specs=[VMEM] * (2 * sets),
        out_specs=HBM,
        scratch_shapes=[pltpu.VMEM(shape, BF16), pltpu.SemaphoreType.DMA((blocks,))],
        compiler_params=limit(8),
    )(*rows, *partials)


def leave(counts, first_level, terms_in, deflation):
    cx, cy, rhs, line = first_level.shape
    slots = deflation.shape[2]

    def body(count, first_level, terms_in, vectors, out, held, basis, made, sems):
        loads = []
        for a in range(cx):
            for b in range(cy):
                for n, (source, place) in enumerate(((vectors, basis), (first_level, held))):
                    copy = pltpu.make_async_copy(source.at[a, b], place.at[a, b], sems.at[n, a, b])
                    copy.start()
                    loads.append(copy)
        total = terms_in[0].astype(F32)
        for i in range(1, terms_in.shape[0]):
            total = total + terms_in[i].astype(F32)
        solved = jnp.where(keep_mask(count, slots, rhs), total, 0.0).astype(BF16)
        saves = []
        for a in range(cx):
            for b in range(cy):
                for n in range(2):
                    loads[2 * (a * cy + b) + n].wait()
                value = lax.dot_general(
                    solved, basis[a, b], (((0,), (0,)), ((), ())), preferred_element_type=F32
                )
                made[a, b] = value + held[a, b]
                copy = pltpu.make_async_copy(made.at[a, b], out.at[a, b], sems.at[2, a, b])
                copy.start()
                saves.append(copy)
        for copy in saves:
            copy.wait()

    return pl.pallas_call(
        body,
        out_shape=struct(first_level.shape, F32),
        in_specs=[SMEM, HBM, VMEM, HBM],
        out_specs=HBM,
        scratch_shapes=[
            pltpu.VMEM(first_level.shape, F32),
            pltpu.VMEM(deflation.shape, deflation.dtype),
            pltpu.VMEM(first_level.shape, F32),
            pltpu.SemaphoreType.DMA((3, cx, cy)),
        ],
        compiler_params=limit(40),
    )(counts, first_level, terms_in, deflation)


def solution(mesh):
    n_grp, n_sub = mesh.shape["grp"], mesh.shape["sub"]
    sizes = {"zh": 2, "x": n_grp // 2, "zl": 2, "y": n_sub // 4, "c": 2}
    fine = Mesh(mesh.devices.reshape([sizes[a] for a in AXES]), AXES)

    def body(residual_field, line_inverse, deflation, counts, coarse_factor):
        tie = lax.optimization_barrier
        width = deflation.shape[2] * sizes["y"] * sizes["c"]

        rounded, to_near, to_far, spread = enter(residual_field, deflation, counts, n_grp * sizes["y"])
        near, far = swap_pairs(to_near, GRP, n_grp, 0), swap_pairs(to_far, GRP, n_grp, 1)
        coarse_factor, _ = tie((coarse_factor, to_near))
        kept, away = cut_factor(coarse_factor, n_grp, width)
        given = swap(away, "zl")
        far, _ = tie((far, kept))
        to_pair, to_outer, own, ends = columns(near, far, rounded)
        outer, pair = swap_outward(to_outer, n_sub), swap(to_pair, "c")
        spread, _ = tie((spread, to_outer))
        gathered = lax.all_to_all(spread, SPREAD, 0, 0)

        windows = (own, ends, pair, outer)
        to_pair, to_outer = rim_lines(windows, line_inverse)
        from_outer, from_pair = swap_outward(to_outer, n_sub), swap(to_pair, "c")
        gathered, kept, given, _ = tie((gathered, kept, given, to_outer))
        rows = (kept, given, swap(kept, "c"), swap(given, "c"))
        partial = lower(rows, gathered)
        partials = (partial, swap(partial, "zl"), swap(partial, "c"), swap_across(partial))
        own, _ = tie((own, partial))
        inner = inner_lines((own, ends, pair, outer), line_inverse)
        partial, own, inner = tie((partial, own, inner))
        terms_out = raise_back(rows, (partial, *partials[1:]))
        terms_in = lax.all_to_all(terms_out, SPREAD, 0, 0)
        own, _ = tie((own, terms_out))
        to_near, to_far = row_lines((own, ends, pair, outer), line_inverse, from_pair, from_outer)
        from_near, from_far = swap_pairs(to_near, GRP, n_grp, 0), swap_pairs(to_far, GRP, n_grp, 1)
        first_level = collect(inner, from_pair, from_outer, from_near, from_far)
        return leave(counts, first_level, terms_in, deflation)

    return jax.shard_map(
        body,
        mesh=fine,
        in_specs=(
            P(GRP, SUB, None, None),
            P(GRP, SUB, None, None, None),
            P(GRP, SUB, None, None),
            P(GRP, SUB),
            P(AXES, None),
        ),
        out_specs=P(GRP, SUB, None, None),
        check_vma=False,
    )
```

```python
import jax
import jax.numpy as jnp
from jax import lax
from jax.experimental import pallas as pl
from jax.experimental.pallas import tpu as pltpu
from jax.sharding import Mesh, PartitionSpec as P

AXES = ("zh", "x", "zl", "y", "c")
GRP = ("zh", "x")
SUB = ("zl", "y", "c")
SPREAD = ("zh", "zl", "y")
RING = "x"

STEPS = ((-1, 0), (0, -1), (0, 0), (0, 1), (1, 0))
WIDE = 4
VMEM = pl.BlockSpec(memory_space=pltpu.VMEM)
SMEM = pl.BlockSpec(memory_space=pltpu.SMEM)
ANY = pl.BlockSpec(memory_space=pl.ANY)
HBM = pl.BlockSpec(memory_space=pltpu.HBM)
MIB = 1024 * 1024
F32 = jnp.float32
BF16 = jnp.bfloat16


def limit(mib):
    return pltpu.CompilerParams(vmem_limit_bytes=mib * MIB)


def struct(shape, dtype):
    return jax.ShapeDtypeStruct(shape, dtype)


def estimate(flops, size):
    return pl.CostEstimate(flops=flops, bytes_accessed=size, transcendentals=0)


def rotate(value, axes, size, step):
    return lax.ppermute(value, axes, [(i, (i + step) % size) for i in range(size)])


def swap(value, axis):
    return lax.ppermute(value, axis, [(0, 1), (1, 0)])


def swap_pairs(value, axes, size, begin):
    pairs = []
    for i in range(begin, size - 1, 2):
        pairs += [(i, i + 1), (i + 1, i)]
    return lax.ppermute(value, axes, pairs)


def swap_outward(value, size):
    pairs = []
    for i in range(1, size, 2):
        pairs += [(i, (i + 1) % size), ((i + 1) % size, i)]
    return lax.ppermute(value, SUB, pairs)


def present(flag, value):
    return jnp.where(flag, value, jnp.zeros_like(value))


def terms(a, b):
    found = []
    for k, (p, q) in enumerate(STEPS):
        if 0 <= a + p < WIDE and 0 <= b + q < WIDE:
            found.append((k, a + p, b + q))
    return found


def position():
    spot = {axis: lax.axis_index(axis) for axis in AXES}
    size = {axis: lax.axis_size(axis) for axis in AXES}
    core, x = spot["c"], spot["x"]
    before = jnp.logical_or(spot["zh"] > 0, x > 0)
    after = jnp.logical_or(spot["zh"] < size["zh"] - 1, x < size["x"] - 1)
    outward = spot["zl"] * size["y"] + spot["y"]
    past = jnp.where(core == 0, outward > 0, outward < size["zl"] * size["y"] - 1)
    return core, before, after, past, lax.rem(x, 2)


def line_kernel(cells, put, fetch, own, ends, pair, outer, blocks, *rest):
    at = position()
    more, (sides, held, sems) = rest[:-3], rest[-3:]
    if fetch:
        window_sems, more = more[-1], more[:-1]
        targets, more = more[-2:], more[:-2]
        loads = []
        for i, (source, target) in enumerate(zip((own, ends), targets)):
            loads.append(pltpu.make_async_copy(source, target, window_sems.at[i]))
            loads[i].start()
        own, ends = targets
    slot, plan = 0, []
    for a, b in cells:
        found = terms(a, b)
        start, run, copies = slot, 0, []
        for i, (k, _, _) in enumerate(found):
            run += 1
            if i + 1 == len(found) or found[i + 1][0] != k + 1:
                source = blocks.at[a, b, pl.ds(k + 1 - run, run)]
                copies.append(pltpu.make_async_copy(source, held.at[pl.ds(slot, run)], sems.at[slot]))
                copies[-1].start()
                slot, run = slot + run, 0
        plan.append((start, copies, found))

    if fetch:
        for load in loads:
            load.wait()
    first = at[0] == 0
    for a in range(WIDE):
        near, far = pair[a, 0], present(at[3], outer[a, 0])
        sides[0, a] = jnp.where(first, far, near)
        sides[1, a] = jnp.where(first, near, far)

    def window(a, b):
        if b == 0:
            return sides[0, a]
        if b == WIDE - 1:
            return sides[1, a]
        if a in (0, WIDE - 1):
            return ends[0 if a == 0 else 1, b - 1]
        return own[a - 1, b - 1]

    line = held.shape[-1]
    for (a, b), (start, copies, found) in zip(cells, plan):
        for copy in copies:
            copy.wait()
        sources = jnp.concatenate([window(sa, sb) for _, sa, sb in found], axis=1)
        weights = held[start : start + len(found)].reshape(len(found) * line, line)
        put(a, b, jnp.dot(sources, weights, preferred_element_type=F32), at, more)


def line_solve(cells, put, shapes, windows, line_inverse, extra=(), fetch=False):
    count = sum(len(terms(a, b)) for a, b in cells)
    line = line_inverse.shape[-1]
    rhs = windows[0].shape[2]

    def body(*refs):
        line_kernel(cells, put, fetch, *refs)

    if fetch:
        shapes = shapes + [struct(w.shape, w.dtype) for w in windows[:2]]
    return pl.pallas_call(
        body,
        out_shape=shapes,
        in_specs=[ANY if fetch else VMEM] * 2 + [VMEM] * 2 + [HBM] + [VMEM] * len(extra),
        out_specs=[VMEM] * len(shapes),
        scratch_shapes=[pltpu.SemaphoreType.DMA((2,))] * fetch
        + [
            pltpu.VMEM((2, WIDE, rhs, line), BF16),
            pltpu.VMEM((count, line, line), line_inverse.dtype),
            pltpu.SemaphoreType.DMA((count,)),
        ],
        compiler_params=limit(42),
        cost_estimate=estimate(2 * count * rhs * line * line, count * line * line * 2),
    )(*windows, line_inverse, *extra)


def put_rim(a, b, value, at, refs):
    value = value.astype(BF16)
    first = at[0] == 0
    to_pair = first if b else jnp.logical_not(first)

    @pl.when(to_pair)
    def _():
        refs[0][a, 0] = value

    @pl.when(jnp.logical_not(to_pair))
    def _():
        refs[1][a, 0] = value


def returned(at, from_pair, from_outer, a, b):
    near, far = from_pair[a, 0], present(at[3], from_outer[a, 0])
    return jnp.where((at[0] == 0) == (b == 1), far, near).astype(F32)


def put_rows(a, b, value, at, refs):
    from_pair, from_outer, near, far = refs
    value = (value + returned(at, from_pair, from_outer, a, b)).astype(BF16)
    to_near = (at[4] == 0) == (a != 0)

    @pl.when(to_near)
    def _():
        near[0, b - 1] = value

    @pl.when(jnp.logical_not(to_near))
    def _():
        far[0, b - 1] = value


def put_inner(a, b, value, at, refs):
    refs[-1][a - 1, b - 1] = value


def columns(near, far, rounded):
    rhs, line = rounded.shape[2:]

    def body(near, far, rounded, pair, outer, own, ends):
        at = position()
        first, even = at[0] == 0, at[4] == 0
        for a in range(WIDE):
            if a in (0, WIDE - 1):
                for b in range(2):
                    low, high = (far, near) if a == 0 else (near, far)
                    ends[a // 2, b] = present(at[1 + a // 2], jnp.where(even, low[0, b], high[0, b]))
                left, right = ends[a // 2, 0], ends[a // 2, 1]
            else:
                left, right = rounded[a - 1, 0], rounded[a - 1, 1]
                own[a - 1, 0], own[a - 1, 1] = left, right
            pair[a, 0] = jnp.where(first, right, left)
            outer[a, 0] = jnp.where(first, left, right)

    out, square = struct((WIDE, 1, rhs, line), BF16), struct(rounded.shape, BF16)
    return pl.pallas_call(
        body,
        out_shape=[out, out, square, square],
        in_specs=[VMEM] * 3,
        out_specs=[VMEM] * 4,
        compiler_params=limit(4),
    )(near, far, rounded)


def rim_lines(windows, line_inverse):
    _, _, rhs, line = windows[0].shape
    column = struct((WIDE, 1, rhs, line), BF16)
    cells = [(a, b) for a in range(WIDE) for b in (0, WIDE - 1)]
    return line_solve(cells, put_rim, [column, column], windows, line_inverse, fetch=True)


def row_lines(windows, line_inverse, from_pair, from_outer):
    _, _, rhs, line = windows[0].shape
    row = struct((1, 2, rhs, line), BF16)
    cells = [(a, b) for a in (0, WIDE - 1) for b in (1, 2)]
    return line_solve(cells, put_rows, [row, row], windows, line_inverse, (from_pair, from_outer))


def inner_lines(windows, line_inverse):
    cells = [(a, b) for a in (1, 2) for b in (1, 2)]
    return line_solve(cells, put_inner, [struct(windows[0].shape, F32)], windows, line_inverse)[0]


def collect(inner, from_pair, from_outer, from_near, from_far):
    cx, cy, _, _ = inner.shape

    def body(inner, from_pair, from_outer, from_near, from_far, out):
        at = position()
        for a in range(cx):
            for b in range(cy):
                side = returned(at, from_pair, from_outer, a + 1, b + 1)
                low, high = (from_far, from_near) if a == 0 else (from_near, from_far)
                across = present(at[1 + a], jnp.where(at[4] == 0, low[0, b], high[0, b])).astype(F32)
                out[a, b] = inner[a, b] + side + across

    return pl.pallas_call(
        body,
        out_shape=struct(inner.shape, F32),
        in_specs=[VMEM] * 5,
        out_specs=VMEM,
        compiler_params=limit(8),
        cost_estimate=estimate(10**9, 4 * 10**6),
    )(inner, from_pair, from_outer, from_near, from_far)


def keep_mask(count, slots, rhs):
    return lax.broadcasted_iota(jnp.int32, (slots, rhs), 0) < count[0, 0]


def round_cells(residual_field):
    cx, cy, rhs, line = residual_field.shape

    def body(residual, rounded, near, far):
        even = position()[4] == 0
        for b in range(cy):
            first, second = residual[0, b].astype(BF16), residual[1, b].astype(BF16)
            rounded[0, b], rounded[1, b] = first, second
            near[0, b] = jnp.where(even, second, first)
            far[0, b] = jnp.where(even, first, second)

    row = struct((1, cy, rhs, line), BF16)
    return pl.pallas_call(
        body,
        out_shape=[struct(residual_field.shape, BF16), row, row],
        in_specs=[VMEM],
        out_specs=[VMEM] * 3,
        compiler_params=limit(4),
    )(residual_field)


def prepare(rounded, deflation, counts, factor, copies, ring, blocks):
    slots, line = deflation.shape[2:]
    cx, cy, rhs, _ = rounded.shape
    width = factor.shape[1] // (ring * blocks)

    def body(count, rounded, vectors, factor, *refs):
        spread, parts = refs[0], refs[1 : 1 + ring]
        made, cut, sems = refs[1 + ring :]
        here = lax.axis_index("x")
        saves = []
        for step in range(ring):
            n = (step + 1) % ring
            there = lax.rem(here + n, ring)
            for j in range(blocks):
                start = pl.multiple_of((j * ring + there) * width, width)
                cut[n, j] = factor[:, pl.ds(start, width)].astype(BF16)
            saves.append(pltpu.make_async_copy(cut.at[n], parts[n], sems.at[n]))
            saves[-1].start()
        total = None
        for a in range(cx):
            for b in range(cy):
                part = lax.dot_general(
                    vectors[a, b], rounded[a, b], (((1,), (1,)), ((), ())), preferred_element_type=F32
                )
                total = part if total is None else total + part
        total = jnp.where(keep_mask(count, slots, rhs), total, 0.0).astype(BF16)
        for i in range(copies):
            made[i] = total
        saves.append(pltpu.make_async_copy(made, spread, sems.at[ring]))
        saves[-1].start()
        for save in saves:
            save.wait()

    return pl.pallas_call(
        body,
        out_shape=[struct((copies, slots, rhs), BF16)] + [struct((blocks, slots, width), BF16)] * ring,
        in_specs=[SMEM, VMEM, VMEM, VMEM],
        out_specs=[HBM] * (1 + ring),
        scratch_shapes=[
            pltpu.VMEM((copies, slots, rhs), BF16),
            pltpu.VMEM((ring, blocks, slots, width), BF16),
            pltpu.SemaphoreType.DMA((1 + ring,)),
        ],
        compiler_params=limit(6),
    )(counts, rounded, deflation, factor)


def halves(value):
    high = value.astype(BF16)
    return high, (value - high.astype(F32)).astype(BF16)


def lower(rows, mine, other):
    sets = len(rows)
    blocks, slots, _ = rows[0].shape
    count, _, rhs = mine.shape
    per = count // blocks

    def body(*refs):
        rows, (mine, other, out) = refs[:sets], refs[sets:]
        first = lax.axis_index("c") == 0
        total = None
        for j in range(blocks):
            pieces = []
            for y in range(per):
                a, b = mine[j * per + y], other[j * per + y]
                pieces += [jnp.where(first, a, b), jnp.where(first, b, a)]
            factor = jnp.concatenate([r[j] for r in rows], 0)
            part = jnp.dot(factor, jnp.concatenate(pieces, 0), preferred_element_type=F32)
            total = part if total is None else total + part
        for n in range(sets):
            out[n] = total[n * slots : (n + 1) * slots]

    return pl.pallas_call(
        body,
        out_shape=struct((sets, slots, rhs), F32),
        in_specs=[VMEM] * (sets + 2),
        out_specs=VMEM,
        compiler_params=limit(8),
    )(*rows, mine, other)


def raise_back(rows, partial, received):
    sets = len(rows)
    blocks, slots, width = rows[0].shape
    rhs = partial.shape[2]
    per = width // (2 * slots)

    def body(*refs):
        rows, partial, received = refs[:sets], refs[sets], refs[sets + 1 : 2 * sets]
        mine, other = refs[2 * sets :]
        first = lax.axis_index("c") == 0
        sums = []
        for n in range(sets):
            total = partial[n]
            for step in range(1, sets):
                total = total + received[step - 1][(n - step) % sets]
            sums.append(total)
        lowered_high, lowered_low = halves(jnp.concatenate(sums, 0))
        over = (((0,), (0,)), ((), ()))
        for j in range(blocks):
            factor = jnp.concatenate([r[j] for r in rows], 0)
            part = lax.dot_general(factor, lowered_high, over, preferred_element_type=F32)
            part = part + lax.dot_general(factor, lowered_low, over, preferred_element_type=F32)
            for y in range(per):
                a = part[2 * y * slots : (2 * y + 1) * slots]
                b = part[(2 * y + 1) * slots : (2 * y + 2) * slots]
                mine[j * per + y] = jnp.where(first, a, b)
                other[j * per + y] = jnp.where(first, b, a).astype(BF16)

    shape = (blocks * per, slots, rhs)
    return pl.pallas_call(
        body,
        out_shape=[struct(shape, F32), struct(shape, BF16)],
        in_specs=[VMEM] * (2 * sets),
        out_specs=[VMEM, VMEM],
        compiler_params=limit(8),
    )(*rows, partial, *received)


def leave(counts, first_level, terms_in, deflation):
    cx, cy, rhs, line = first_level.shape
    slots = deflation.shape[2]

    def body(count, first_level, terms_in, vectors, out, held, basis, made, sems):
        loads = []
        for a in range(cx):
            for b in range(cy):
                for n, (source, place) in enumerate(((vectors, basis), (first_level, held))):
                    copy = pltpu.make_async_copy(source.at[a, b], place.at[a, b], sems.at[n, a, b])
                    copy.start()
                    loads.append(copy)
        total = terms_in[0].astype(F32)
        for i in range(1, terms_in.shape[0]):
            total = total + terms_in[i].astype(F32)
        solved = jnp.where(keep_mask(count, slots, rhs), total, 0.0).astype(BF16)
        saves = []
        for a in range(cx):
            for b in range(cy):
                for n in range(2):
                    loads[2 * (a * cy + b) + n].wait()
                value = lax.dot_general(
                    solved, basis[a, b], (((0,), (0,)), ((), ())), preferred_element_type=F32
                )
                made[a, b] = value + held[a, b]
                copy = pltpu.make_async_copy(made.at[a, b], out.at[a, b], sems.at[2, a, b])
                copy.start()
                saves.append(copy)
        for copy in saves:
            copy.wait()

    return pl.pallas_call(
        body,
        out_shape=struct(first_level.shape, F32),
        in_specs=[SMEM, HBM, VMEM, HBM],
        out_specs=HBM,
        scratch_shapes=[
            pltpu.VMEM(first_level.shape, F32),
            pltpu.VMEM(deflation.shape, deflation.dtype),
            pltpu.VMEM(first_level.shape, F32),
            pltpu.SemaphoreType.DMA((3, cx, cy)),
        ],
        compiler_params=limit(40),
    )(counts, first_level, terms_in, deflation)


def solution(mesh):
    n_grp, n_sub = mesh.shape["grp"], mesh.shape["sub"]
    sizes = {"zh": 2, "x": n_grp // 2, "zl": 2, "y": n_sub // 4, "c": 2}
    fine = Mesh(mesh.devices.reshape([sizes[a] for a in AXES]), AXES)

    def body(residual_field, line_inverse, deflation, counts, coarse_factor):
        tie = lax.optimization_barrier
        ring = sizes["x"]

        rounded, to_near, to_far = round_cells(residual_field)
        near, far = swap_pairs(to_near, GRP, n_grp, 0), swap_pairs(to_far, GRP, n_grp, 1)
        receivers = sizes["zh"] * sizes["zl"] * sizes["y"]
        spread, *parts = prepare(rounded, deflation, counts, coarse_factor, receivers, ring, sizes["zh"])
        rows = [parts[0]] + [rotate(parts[n], RING, ring, n) for n in range(1, ring)]
        far, _ = tie((far, parts[0]))
        to_pair, to_outer, own, ends = columns(near, far, rounded)
        outer, pair = swap_outward(to_outer, n_sub), swap(to_pair, "c")
        spread, _ = tie((spread, to_outer))
        gathered = lax.all_to_all(spread, SPREAD, 0, 0)
        outer, *rows = tie((outer, *rows))

        to_pair, to_outer, own, ends = rim_lines((own, ends, pair, outer), line_inverse)
        from_outer, from_pair = swap_outward(to_outer, n_sub), swap(to_pair, "c")
        gathered, _ = tie((gathered, to_outer))
        partial = lower(rows, gathered, swap(gathered, "c"))
        received = [rotate(partial, RING, ring, n) for n in range(1, ring)]
        own, _ = tie((own, partial))
        to_near, to_far = row_lines((own, ends, pair, outer), line_inverse, from_pair, from_outer)
        partial, _ = tie((partial, to_near))
        own_terms, other_terms = raise_back(rows, partial, received)
        to_near, to_far, other_terms = tie((to_near, to_far, other_terms))
        from_near, from_far = swap_pairs(to_near, GRP, n_grp, 0), swap_pairs(to_far, GRP, n_grp, 1)
        own_terms, from_near = tie((own_terms, from_near))
        terms_out = (own_terms + swap(other_terms, "c").astype(F32)).astype(BF16)
        terms_in = lax.all_to_all(terms_out, SPREAD, 0, 0)
        own, _ = tie((own, terms_out))
        inner = inner_lines((own, ends, pair, outer), line_inverse)
        first_level = collect(inner, from_pair, from_outer, from_near, from_far)
        return leave(counts, first_level, terms_in, deflation)

    return jax.shard_map(
        body,
        mesh=fine,
        in_specs=(
            P(GRP, SUB, None, None),
            P(GRP, SUB, None, None, None),
            P(GRP, SUB, None, None),
            P(GRP, SUB),
            P(AXES, None),
        ),
        out_specs=P(GRP, SUB, None, None),
        check_vma=False,
    )
```

```python
import jax
import jax.numpy as jnp
from jax import lax
from jax.experimental import pallas as pl
from jax.experimental.pallas import tpu as pltpu
from jax.sharding import Mesh, PartitionSpec as P

AXES = ("zh", "x", "zl", "y", "c")
GRP = ("zh", "x")
SUB = ("zl", "y", "c")
SPREAD = ("zh", "zl", "y")
RING = "x"

STEPS = ((-1, 0), (0, -1), (0, 0), (0, 1), (1, 0))
WIDE = 4
VMEM = pl.BlockSpec(memory_space=pltpu.VMEM)
SMEM = pl.BlockSpec(memory_space=pltpu.SMEM)
ANY = pl.BlockSpec(memory_space=pl.ANY)
HBM = pl.BlockSpec(memory_space=pltpu.HBM)
MIB = 1024 * 1024
F32 = jnp.float32
BF16 = jnp.bfloat16


def limit(mib):
    return pltpu.CompilerParams(vmem_limit_bytes=mib * MIB)


def struct(shape, dtype):
    return jax.ShapeDtypeStruct(shape, dtype)


def estimate(flops, size):
    return pl.CostEstimate(flops=flops, bytes_accessed=size, transcendentals=0)


def rotate(value, axes, size, step):
    return lax.ppermute(value, axes, [(i, (i + step) % size) for i in range(size)])


def swap(value, axis):
    return lax.ppermute(value, axis, [(0, 1), (1, 0)])


def swap_pairs(value, axes, size, begin):
    pairs = []
    for i in range(begin, size - 1, 2):
        pairs += [(i, i + 1), (i + 1, i)]
    return lax.ppermute(value, axes, pairs)


def swap_outward(value, size):
    pairs = []
    for i in range(1, size, 2):
        pairs += [(i, (i + 1) % size), ((i + 1) % size, i)]
    return lax.ppermute(value, SUB, pairs)


def present(flag, value):
    return jnp.where(flag, value, jnp.zeros_like(value))


def terms(a, b):
    found = []
    for k, (p, q) in enumerate(STEPS):
        if 0 <= a + p < WIDE and 0 <= b + q < WIDE:
            found.append((k, a + p, b + q))
    return found


def position():
    spot = {axis: lax.axis_index(axis) for axis in AXES}
    size = {axis: lax.axis_size(axis) for axis in AXES}
    core, x = spot["c"], spot["x"]
    before = jnp.logical_or(spot["zh"] > 0, x > 0)
    after = jnp.logical_or(spot["zh"] < size["zh"] - 1, x < size["x"] - 1)
    outward = spot["zl"] * size["y"] + spot["y"]
    past = jnp.where(core == 0, outward > 0, outward < size["zl"] * size["y"] - 1)
    return core, before, after, past, lax.rem(x, 2)


def line_kernel(cells, put, fetch, own, ends, pair, outer, blocks, *rest):
    at = position()
    more, (sides, held, sems) = rest[:-3], rest[-3:]
    if fetch:
        window_sems, more = more[-1], more[:-1]
        targets, more = more[-2:], more[:-2]
        loads = []
        for i, (source, target) in enumerate(zip((own, ends), targets)):
            loads.append(pltpu.make_async_copy(source, target, window_sems.at[i]))
            loads[i].start()
        own, ends = targets
    slot, plan = 0, []
    for a, b in cells:
        found = terms(a, b)
        start, run, copies = slot, 0, []
        for i, (k, _, _) in enumerate(found):
            run += 1
            if i + 1 == len(found) or found[i + 1][0] != k + 1:
                source = blocks.at[a, b, pl.ds(k + 1 - run, run)]
                copies.append(pltpu.make_async_copy(source, held.at[pl.ds(slot, run)], sems.at[slot]))
                copies[-1].start()
                slot, run = slot + run, 0
        plan.append((start, copies, found))

    first = at[0] == 0
    for a in range(WIDE):
        near, far = pair[a, 0], present(at[3], outer[a, 0])
        sides[0, a] = jnp.where(first, far, near)
        sides[1, a] = jnp.where(first, near, far)

    if fetch:
        for load in loads:
            load.wait()

    def window(a, b):
        if b == 0:
            return sides[0, a]
        if b == WIDE - 1:
            return sides[1, a]
        if a in (0, WIDE - 1):
            return ends[0 if a == 0 else 1, b - 1]
        return own[a - 1, b - 1]

    line = held.shape[-1]
    for (a, b), (start, copies, found) in zip(cells, plan):
        for copy in copies:
            copy.wait()
        sources = jnp.concatenate([window(sa, sb) for _, sa, sb in found], axis=1)
        weights = held[start : start + len(found)].reshape(len(found) * line, line)
        put(a, b, jnp.dot(sources, weights, preferred_element_type=F32), at, more)


def line_solve(cells, put, shapes, windows, line_inverse, extra=(), fetch=False):
    count = sum(len(terms(a, b)) for a, b in cells)
    line = line_inverse.shape[-1]
    rhs = windows[0].shape[2]

    def body(*refs):
        line_kernel(cells, put, fetch, *refs)

    if fetch:
        shapes = shapes + [struct(w.shape, w.dtype) for w in windows[:2]]
    return pl.pallas_call(
        body,
        out_shape=shapes,
        in_specs=[ANY if fetch else VMEM] * 2 + [VMEM] * 2 + [HBM] + [VMEM] * len(extra),
        out_specs=[VMEM] * len(shapes),
        scratch_shapes=[pltpu.SemaphoreType.DMA((2,))] * fetch
        + [
            pltpu.VMEM((2, WIDE, rhs, line), BF16),
            pltpu.VMEM((count, line, line), line_inverse.dtype),
            pltpu.SemaphoreType.DMA((count,)),
        ],
        compiler_params=limit(42),
        cost_estimate=estimate(2 * count * rhs * line * line, count * line * line * 2),
    )(*windows, line_inverse, *extra)


def put_rim(a, b, value, at, refs):
    value = value.astype(BF16)
    first = at[0] == 0
    to_pair = first if b else jnp.logical_not(first)

    @pl.when(to_pair)
    def _():
        refs[0][a, 0] = value

    @pl.when(jnp.logical_not(to_pair))
    def _():
        refs[1][a, 0] = value


def returned(at, from_pair, from_outer, a, b):
    near, far = from_pair[a, 0], present(at[3], from_outer[a, 0])
    return jnp.where((at[0] == 0) == (b == 1), far, near).astype(F32)


def put_rows(a, b, value, at, refs):
    from_pair, from_outer, near, far = refs
    value = (value + returned(at, from_pair, from_outer, a, b)).astype(BF16)
    to_near = (at[4] == 0) == (a != 0)

    @pl.when(to_near)
    def _():
        near[0, b - 1] = value

    @pl.when(jnp.logical_not(to_near))
    def _():
        far[0, b - 1] = value


def put_inner(a, b, value, at, refs):
    refs[-1][a - 1, b - 1] = value


def columns(near, far, rounded):
    rhs, line = rounded.shape[2:]

    def body(near, far, rounded, pair, outer, own, ends):
        at = position()
        first, even = at[0] == 0, at[4] == 0
        for a in range(WIDE):
            if a in (0, WIDE - 1):
                for b in range(2):
                    low, high = (far, near) if a == 0 else (near, far)
                    ends[a // 2, b] = present(at[1 + a // 2], jnp.where(even, low[0, b], high[0, b]))
                left, right = ends[a // 2, 0], ends[a // 2, 1]
            else:
                left, right = rounded[a - 1, 0], rounded[a - 1, 1]
                own[a - 1, 0], own[a - 1, 1] = left, right
            pair[a, 0] = jnp.where(first, right, left)
            outer[a, 0] = jnp.where(first, left, right)

    out, square = struct((WIDE, 1, rhs, line), BF16), struct(rounded.shape, BF16)
    return pl.pallas_call(
        body,
        out_shape=[out, out, square, square],
        in_specs=[VMEM] * 3,
        out_specs=[VMEM] * 4,
        compiler_params=limit(4),
    )(near, far, rounded)


def rim_lines(windows, line_inverse):
    _, _, rhs, line = windows[0].shape
    column = struct((WIDE, 1, rhs, line), BF16)
    cells = [(a, b) for a in range(WIDE) for b in (0, WIDE - 1)]
    return line_solve(cells, put_rim, [column, column], windows, line_inverse, fetch=True)


def row_lines(windows, line_inverse, from_pair, from_outer):
    _, _, rhs, line = windows[0].shape
    row = struct((1, 2, rhs, line), BF16)
    cells = [(a, b) for a in (0, WIDE - 1) for b in (1, 2)]
    return line_solve(cells, put_rows, [row, row], windows, line_inverse, (from_pair, from_outer))


def inner_lines(windows, line_inverse):
    cells = [(a, b) for a in (1, 2) for b in (1, 2)]
    return line_solve(cells, put_inner, [struct(windows[0].shape, F32)], windows, line_inverse)[0]


def collect(inner, from_pair, from_outer, from_near, from_far):
    cx, cy, _, _ = inner.shape

    def body(inner, from_pair, from_outer, from_near, from_far, out):
        at = position()
        for a in range(cx):
            for b in range(cy):
                side = returned(at, from_pair, from_outer, a + 1, b + 1)
                low, high = (from_far, from_near) if a == 0 else (from_near, from_far)
                across = present(at[1 + a], jnp.where(at[4] == 0, low[0, b], high[0, b])).astype(F32)
                out[a, b] = inner[a, b] + side + across

    return pl.pallas_call(
        body,
        out_shape=struct(inner.shape, F32),
        in_specs=[VMEM] * 5,
        out_specs=VMEM,
        compiler_params=limit(8),
        cost_estimate=estimate(10**9, 4 * 10**6),
    )(inner, from_pair, from_outer, from_near, from_far)


def keep_mask(count, slots, rhs):
    return lax.broadcasted_iota(jnp.int32, (slots, rhs), 0) < count[0, 0]


def round_cells(residual_field):
    cx, cy, rhs, line = residual_field.shape

    def body(residual, rounded, near, far):
        even = position()[4] == 0
        for b in range(cy):
            first, second = residual[0, b].astype(BF16), residual[1, b].astype(BF16)
            rounded[0, b], rounded[1, b] = first, second
            near[0, b] = jnp.where(even, second, first)
            far[0, b] = jnp.where(even, first, second)

    row = struct((1, cy, rhs, line), BF16)
    return pl.pallas_call(
        body,
        out_shape=[struct(residual_field.shape, BF16), row, row],
        in_specs=[VMEM],
        out_specs=[VMEM] * 3,
        compiler_params=limit(4),
    )(residual_field)


def prepare(rounded, deflation, counts, factor, copies, ring, blocks):
    slots, line = deflation.shape[2:]
    cx, cy, rhs, _ = rounded.shape
    width = factor.shape[1] // (ring * blocks)

    def body(count, rounded, vectors, factor, *refs):
        spread, parts = refs[0], refs[1 : 1 + ring]
        made, cut, sems = refs[1 + ring :]
        here = lax.axis_index("x")
        saves = []
        for step in range(ring):
            n = (step + 1) % ring
            there = lax.rem(here + n, ring)
            for j in range(blocks):
                start = pl.multiple_of((j * ring + there) * width, width)
                cut[n, j] = factor[:, pl.ds(start, width)].astype(BF16)
            saves.append(pltpu.make_async_copy(cut.at[n], parts[n], sems.at[n]))
            saves[-1].start()
        total = None
        for a in range(cx):
            for b in range(cy):
                part = lax.dot_general(
                    vectors[a, b], rounded[a, b], (((1,), (1,)), ((), ())), preferred_element_type=F32
                )
                total = part if total is None else total + part
        total = jnp.where(keep_mask(count, slots, rhs), total, 0.0).astype(BF16)
        for i in range(copies):
            made[i] = total
        saves.append(pltpu.make_async_copy(made, spread, sems.at[ring]))
        saves[-1].start()
        for save in saves:
            save.wait()

    return pl.pallas_call(
        body,
        out_shape=[struct((copies, slots, rhs), BF16)] + [struct((blocks, slots, width), BF16)] * ring,
        in_specs=[SMEM, VMEM, VMEM, VMEM],
        out_specs=[HBM] * (1 + ring),
        scratch_shapes=[
            pltpu.VMEM((copies, slots, rhs), BF16),
            pltpu.VMEM((ring, blocks, slots, width), BF16),
            pltpu.SemaphoreType.DMA((1 + ring,)),
        ],
        compiler_params=limit(6),
    )(counts, rounded, deflation, factor)


def halves(value):
    high = value.astype(BF16)
    return high, (value - high.astype(F32)).astype(BF16)


def lower(rows, mine, other):
    sets = len(rows)
    blocks, slots, _ = rows[0].shape
    count, _, rhs = mine.shape
    per = count // blocks

    def body(*refs):
        rows, (mine, other, out) = refs[:sets], refs[sets:]
        first = lax.axis_index("c") == 0
        total = None
        for j in range(blocks):
            pieces = []
            for y in range(per):
                a, b = mine[j * per + y], other[j * per + y]
                pieces += [jnp.where(first, a, b), jnp.where(first, b, a)]
            factor = jnp.concatenate([r[j] for r in rows], 0)
            part = jnp.dot(factor, jnp.concatenate(pieces, 0), preferred_element_type=F32)
            total = part if total is None else total + part
        for n in range(sets):
            out[n] = total[n * slots : (n + 1) * slots]

    return pl.pallas_call(
        body,
        out_shape=struct((sets, slots, rhs), F32),
        in_specs=[VMEM] * (sets + 2),
        out_specs=VMEM,
        compiler_params=limit(8),
    )(*rows, mine, other)


def raise_back(rows, partial, received):
    sets = len(rows)
    blocks, slots, width = rows[0].shape
    rhs = partial.shape[2]
    per = width // (2 * slots)

    def body(*refs):
        rows, partial, received = refs[:sets], refs[sets], refs[sets + 1 : 2 * sets]
        mine, other = refs[2 * sets :]
        first = lax.axis_index("c") == 0
        sums = []
        for n in range(sets):
            total = partial[n]
            for step in range(1, sets):
                total = total + received[step - 1][(n - step) % sets]
            sums.append(total)
        lowered_high, lowered_low = halves(jnp.concatenate(sums, 0))
        over = (((0,), (0,)), ((), ()))
        for j in range(blocks):
            factor = jnp.concatenate([r[j] for r in rows], 0)
            part = lax.dot_general(factor, lowered_high, over, preferred_element_type=F32)
            part = part + lax.dot_general(factor, lowered_low, over, preferred_element_type=F32)
            for y in range(per):
                a = part[2 * y * slots : (2 * y + 1) * slots]
                b = part[(2 * y + 1) * slots : (2 * y + 2) * slots]
                mine[j * per + y] = jnp.where(first, a, b)
                other[j * per + y] = jnp.where(first, b, a).astype(BF16)

    shape = (blocks * per, slots, rhs)
    return pl.pallas_call(
        body,
        out_shape=[struct(shape, F32), struct(shape, BF16)],
        in_specs=[VMEM] * (2 * sets),
        out_specs=[VMEM, VMEM],
        compiler_params=limit(8),
    )(*rows, partial, *received)


def leave(counts, first_level, terms_in, deflation):
    cx, cy, rhs, line = first_level.shape
    slots = deflation.shape[2]

    def body(count, first_level, terms_in, vectors, out, made, sems):
        total = terms_in[0].astype(F32)
        for i in range(1, terms_in.shape[0]):
            total = total + terms_in[i].astype(F32)
        solved = jnp.where(keep_mask(count, slots, rhs), total, 0.0).astype(BF16)
        saves = []
        for a in range(cx):
            for b in range(cy):
                value = lax.dot_general(
                    solved, vectors[a, b], (((0,), (0,)), ((), ())), preferred_element_type=F32
                )
                made[a, b] = value + first_level[a, b]
                saves.append(pltpu.make_async_copy(made.at[a, b], out.at[a, b], sems.at[a, b]))
                saves[-1].start()
        for save in saves:
            save.wait()

    return pl.pallas_call(
        body,
        out_shape=struct(first_level.shape, F32),
        in_specs=[SMEM, VMEM, VMEM, VMEM],
        out_specs=HBM,
        scratch_shapes=[pltpu.VMEM(first_level.shape, F32), pltpu.SemaphoreType.DMA((cx, cy))],
        compiler_params=limit(6),
    )(counts, first_level, terms_in, deflation)


def solution(mesh):
    n_grp, n_sub = mesh.shape["grp"], mesh.shape["sub"]
    sizes = {"zh": 2, "x": n_grp // 2, "zl": 2, "y": n_sub // 4, "c": 2}
    fine = Mesh(mesh.devices.reshape([sizes[a] for a in AXES]), AXES)

    def body(residual_field, line_inverse, deflation, counts, coarse_factor):
        tie = lax.optimization_barrier
        ring = sizes["x"]

        rounded, to_near, to_far = round_cells(residual_field)
        near, far = swap_pairs(to_near, GRP, n_grp, 0), swap_pairs(to_far, GRP, n_grp, 1)
        receivers = sizes["zh"] * sizes["zl"] * sizes["y"]
        spread, *parts = prepare(rounded, deflation, counts, coarse_factor, receivers, ring, sizes["zh"])
        rows = [parts[0]] + [rotate(parts[n], RING, ring, n) for n in range(1, ring)]
        far, _ = tie((far, parts[0]))
        to_pair, to_outer, own, ends = columns(near, far, rounded)
        outer, pair = swap_outward(to_outer, n_sub), swap(to_pair, "c")
        spread, _ = tie((spread, to_outer))
        gathered = lax.all_to_all(spread, SPREAD, 0, 0)
        outer, *rows = tie((outer, *rows))

        to_pair, to_outer, own, ends = rim_lines((own, ends, pair, outer), line_inverse)
        from_outer, from_pair = swap_outward(to_outer, n_sub), swap(to_pair, "c")
        gathered, _ = tie((gathered, to_outer))
        partial = lower(rows, gathered, swap(gathered, "c"))
        received = [rotate(partial, RING, ring, n) for n in range(1, ring)]
        own, _ = tie((own, partial))
        to_near, to_far = row_lines((own, ends, pair, outer), line_inverse, from_pair, from_outer)
        partial, _ = tie((partial, to_near))
        own_terms, other_terms = raise_back(rows, partial, received)
        to_near, to_far, other_terms = tie((to_near, to_far, other_terms))
        from_near, from_far = swap_pairs(to_near, GRP, n_grp, 0), swap_pairs(to_far, GRP, n_grp, 1)
        terms_out = (own_terms + swap(other_terms, "c").astype(F32)).astype(BF16)
        terms_in = lax.all_to_all(terms_out, SPREAD, 0, 0)
        own, _ = tie((own, terms_out))
        inner = inner_lines((own, ends, pair, outer), line_inverse)
        first_level = collect(inner, from_pair, from_outer, from_near, from_far)
        return leave(counts, first_level, terms_in, deflation)

    return jax.shard_map(
        body,
        mesh=fine,
        in_specs=(
            P(GRP, SUB, None, None),
            P(GRP, SUB, None, None, None),
            P(GRP, SUB, None, None),
            P(GRP, SUB),
            P(AXES, None),
        ),
        out_specs=P(GRP, SUB, None, None),
        check_vma=False,
    )
```

```python
import jax
import jax.numpy as jnp
from jax import lax
from jax.experimental import pallas as pl
from jax.experimental.pallas import tpu as pltpu
from jax.sharding import Mesh, PartitionSpec as P

AXES = ("zh", "x", "zl", "y", "c")
GRP = ("zh", "x")
SUB = ("zl", "y", "c")
SPREAD = ("zh", "zl", "y")
RING = "x"

STEPS = ((-1, 0), (0, -1), (0, 0), (0, 1), (1, 0))
WIDE = 4
VMEM = pl.BlockSpec(memory_space=pltpu.VMEM)
SMEM = pl.BlockSpec(memory_space=pltpu.SMEM)
ANY = pl.BlockSpec(memory_space=pl.ANY)
HBM = pl.BlockSpec(memory_space=pltpu.HBM)
MIB = 1024 * 1024
F32 = jnp.float32
BF16 = jnp.bfloat16


def limit(mib):
    return pltpu.CompilerParams(vmem_limit_bytes=mib * MIB)


def struct(shape, dtype):
    return jax.ShapeDtypeStruct(shape, dtype)


def estimate(flops, size):
    return pl.CostEstimate(flops=flops, bytes_accessed=size, transcendentals=0)


def rotate(value, axes, size, step):
    return lax.ppermute(value, axes, [(i, (i + step) % size) for i in range(size)])


def swap(value, axis):
    return lax.ppermute(value, axis, [(0, 1), (1, 0)])


def swap_pairs(value, axes, size, begin):
    pairs = []
    for i in range(begin, size - 1, 2):
        pairs += [(i, i + 1), (i + 1, i)]
    return lax.ppermute(value, axes, pairs)


def swap_outward(value, size):
    pairs = []
    for i in range(1, size, 2):
        pairs += [(i, (i + 1) % size), ((i + 1) % size, i)]
    return lax.ppermute(value, SUB, pairs)


def present(flag, value):
    return jnp.where(flag, value, jnp.zeros_like(value))


def terms(a, b):
    found = []
    for k, (p, q) in enumerate(STEPS):
        if 0 <= a + p < WIDE and 0 <= b + q < WIDE:
            found.append((k, a + p, b + q))
    return found


def position():
    spot = {axis: lax.axis_index(axis) for axis in AXES}
    size = {axis: lax.axis_size(axis) for axis in AXES}
    core, x = spot["c"], spot["x"]
    before = jnp.logical_or(spot["zh"] > 0, x > 0)
    after = jnp.logical_or(spot["zh"] < size["zh"] - 1, x < size["x"] - 1)
    outward = spot["zl"] * size["y"] + spot["y"]
    past = jnp.where(core == 0, outward > 0, outward < size["zl"] * size["y"] - 1)
    return core, before, after, past, lax.rem(x, 2)


def line_kernel(cells, put, fetch, own, ends, pair, outer, blocks, *rest):
    at = position()
    more, (sides, held, sems) = rest[:-3], rest[-3:]
    if fetch:
        (window_sems, stage, stage_sems), targets, outs = more[-3:], more[-5:-3], more[:-5]
        more = (outs, stage, stage_sems)
        loads = []
        for i, (source, target) in enumerate(zip((own, ends), targets)):
            loads.append(pltpu.make_async_copy(source, target, window_sems.at[i]))
            loads[i].start()
        own, ends = targets
    slot, plan = 0, []
    for a, b in cells:
        found = terms(a, b)
        start, run, copies = slot, 0, []
        for i, (k, _, _) in enumerate(found):
            run += 1
            if i + 1 == len(found) or found[i + 1][0] != k + 1:
                source = blocks.at[a, b, pl.ds(k + 1 - run, run)]
                copies.append(pltpu.make_async_copy(source, held.at[pl.ds(slot, run)], sems.at[slot]))
                copies[-1].start()
                slot, run = slot + run, 0
        plan.append((start, copies, found))

    first = at[0] == 0
    for a in range(WIDE):
        near, far = pair[a, 0], present(at[3], outer[a, 0])
        sides[0, a] = jnp.where(first, far, near)
        sides[1, a] = jnp.where(first, near, far)
    if fetch:
        for load in loads:
            load.wait()

    def window(a, b):
        if b == 0:
            return sides[0, a]
        if b == WIDE - 1:
            return sides[1, a]
        if a in (0, WIDE - 1):
            return ends[0 if a == 0 else 1, b - 1]
        return own[a - 1, b - 1]

    line = held.shape[-1]
    for (a, b), (start, copies, found) in zip(cells, plan):
        for copy in copies:
            copy.wait()
        sources = jnp.concatenate([window(sa, sb) for _, sa, sb in found], axis=1)
        weights = held[start : start + len(found)].reshape(len(found) * line, line)
        put(a, b, jnp.dot(sources, weights, preferred_element_type=F32), at, more)
    if fetch:
        for i in range(2):
            for a in range(WIDE):
                pltpu.make_async_copy(stage.at[i, a], outs[i].at[a, 0], stage_sems.at[i, a]).wait()


def line_solve(cells, put, shapes, windows, line_inverse, extra=(), fetch=False):
    count = sum(len(terms(a, b)) for a, b in cells)
    line = line_inverse.shape[-1]
    rhs = windows[0].shape[2]

    def body(*refs):
        line_kernel(cells, put, fetch, *refs)

    out_specs, scratch = [VMEM] * len(shapes), []
    if fetch:
        shapes = shapes + [struct(w.shape, w.dtype) for w in windows[:2]]
        out_specs = [HBM] * 2 + [VMEM] * 2
        scratch = [
            pltpu.SemaphoreType.DMA((2,)),
            pltpu.VMEM((2, WIDE, rhs, line), BF16),
            pltpu.SemaphoreType.DMA((2, WIDE)),
        ]
    return pl.pallas_call(
        body,
        out_shape=shapes,
        in_specs=[ANY if fetch else VMEM] * 2 + [VMEM] * 2 + [HBM] + [VMEM] * len(extra),
        out_specs=out_specs,
        scratch_shapes=scratch
        + [
            pltpu.VMEM((2, WIDE, rhs, line), BF16),
            pltpu.VMEM((count, line, line), line_inverse.dtype),
            pltpu.SemaphoreType.DMA((count,)),
        ],
        compiler_params=limit(42),
        cost_estimate=estimate(2 * count * rhs * line * line, count * line * line * 2),
    )(*windows, line_inverse, *extra)


def put_rim(a, b, value, at, refs):
    outs, stage, sems = refs
    value = value.astype(BF16)
    first = at[0] == 0
    to_pair = first if b else jnp.logical_not(first)
    for i, chosen in ((0, to_pair), (1, jnp.logical_not(to_pair))):

        @pl.when(chosen)
        def _(i=i):
            stage[i, a] = value
            pltpu.make_async_copy(stage.at[i, a], outs[i].at[a, 0], sems.at[i, a]).start()


def returned(at, from_pair, from_outer, a, b):
    near, far = from_pair[a, 0], present(at[3], from_outer[a, 0])
    return jnp.where((at[0] == 0) == (b == 1), far, near).astype(F32)


def put_rows(a, b, value, at, refs):
    from_pair, from_outer, near, far = refs
    value = (value + returned(at, from_pair, from_outer, a, b)).astype(BF16)
    to_near = (at[4] == 0) == (a != 0)

    @pl.when(to_near)
    def _():
        near[0, b - 1] = value

    @pl.when(jnp.logical_not(to_near))
    def _():
        far[0, b - 1] = value


def put_inner(a, b, value, at, refs):
    refs[-1][a - 1, b - 1] = value


def columns(near, far, rounded):
    rhs, line = rounded.shape[2:]

    def body(near, far, rounded, pair, outer, own, ends):
        at = position()
        first, even = at[0] == 0, at[4] == 0
        for a in range(WIDE):
            if a in (0, WIDE - 1):
                for b in range(2):
                    low, high = (far, near) if a == 0 else (near, far)
                    ends[a // 2, b] = present(at[1 + a // 2], jnp.where(even, low[0, b], high[0, b]))
                left, right = ends[a // 2, 0], ends[a // 2, 1]
            else:
                left, right = rounded[a - 1, 0], rounded[a - 1, 1]
                own[a - 1, 0], own[a - 1, 1] = left, right
            pair[a, 0] = jnp.where(first, right, left)
            outer[a, 0] = jnp.where(first, left, right)

    out, square = struct((WIDE, 1, rhs, line), BF16), struct(rounded.shape, BF16)
    return pl.pallas_call(
        body,
        out_shape=[out, out, square, square],
        in_specs=[VMEM] * 3,
        out_specs=[VMEM] * 4,
        compiler_params=limit(4),
    )(near, far, rounded)


def rim_lines(windows, line_inverse):
    _, _, rhs, line = windows[0].shape
    column = struct((WIDE, 1, rhs, line), BF16)
    cells = [(a, b) for a in range(WIDE) for b in (0, WIDE - 1)]
    return line_solve(cells, put_rim, [column, column], windows, line_inverse, fetch=True)


def row_lines(windows, line_inverse, from_pair, from_outer):
    _, _, rhs, line = windows[0].shape
    row = struct((1, 2, rhs, line), BF16)
    cells = [(a, b) for a in (0, WIDE - 1) for b in (1, 2)]
    return line_solve(cells, put_rows, [row, row], windows, line_inverse, (from_pair, from_outer))


def inner_lines(windows, line_inverse):
    cells = [(a, b) for a in (1, 2) for b in (1, 2)]
    return line_solve(cells, put_inner, [struct(windows[0].shape, F32)], windows, line_inverse)[0]


def collect(inner, from_pair, from_outer, from_near, from_far):
    cx, cy, _, _ = inner.shape

    def body(inner, from_pair, from_outer, from_near, from_far, out):
        at = position()
        for a in range(cx):
            for b in range(cy):
                side = returned(at, from_pair, from_outer, a + 1, b + 1)
                low, high = (from_far, from_near) if a == 0 else (from_near, from_far)
                across = present(at[1 + a], jnp.where(at[4] == 0, low[0, b], high[0, b])).astype(F32)
                out[a, b] = inner[a, b] + side + across

    return pl.pallas_call(
        body,
        out_shape=struct(inner.shape, F32),
        in_specs=[VMEM] * 5,
        out_specs=VMEM,
        compiler_params=limit(8),
        cost_estimate=estimate(10**9, 4 * 10**6),
    )(inner, from_pair, from_outer, from_near, from_far)


def keep_mask(count, slots, rhs):
    return lax.broadcasted_iota(jnp.int32, (slots, rhs), 0) < count[0, 0]


def round_cells(residual_field):
    cx, cy, rhs, line = residual_field.shape

    def body(residual, rounded, near, far):
        even = position()[4] == 0
        for b in range(cy):
            first, second = residual[0, b].astype(BF16), residual[1, b].astype(BF16)
            rounded[0, b], rounded[1, b] = first, second
            near[0, b] = jnp.where(even, second, first)
            far[0, b] = jnp.where(even, first, second)

    row = struct((1, cy, rhs, line), BF16)
    return pl.pallas_call(
        body,
        out_shape=[struct(residual_field.shape, BF16), row, row],
        in_specs=[VMEM],
        out_specs=[VMEM] * 3,
        compiler_params=limit(4),
    )(residual_field)


def prepare(rounded, deflation, counts, factor, copies, ring, blocks):
    slots, line = deflation.shape[2:]
    cx, cy, rhs, _ = rounded.shape
    width = factor.shape[1] // (ring * blocks)

    def body(count, rounded, vectors, factor, *refs):
        spread, parts = refs[0], refs[1 : 1 + ring]
        made, cut, sems = refs[1 + ring :]
        here = lax.axis_index("x")
        saves = []
        for step in range(ring):
            n = (step + 1) % ring
            there = lax.rem(here + n, ring)
            for j in range(blocks):
                start = pl.multiple_of((j * ring + there) * width, width)
                cut[n, j] = factor[:, pl.ds(start, width)].astype(BF16)
            saves.append(pltpu.make_async_copy(cut.at[n], parts[n], sems.at[n]))
            saves[-1].start()
        total = None
        for a in range(cx):
            for b in range(cy):
                part = lax.dot_general(
                    vectors[a, b], rounded[a, b], (((1,), (1,)), ((), ())), preferred_element_type=F32
                )
                total = part if total is None else total + part
        total = jnp.where(keep_mask(count, slots, rhs), total, 0.0).astype(BF16)
        for i in range(copies):
            made[i] = total
        saves.append(pltpu.make_async_copy(made, spread, sems.at[ring]))
        saves[-1].start()
        for save in saves:
            save.wait()

    return pl.pallas_call(
        body,
        out_shape=[struct((copies, slots, rhs), BF16)] + [struct((blocks, slots, width), BF16)] * ring,
        in_specs=[SMEM, VMEM, VMEM, VMEM],
        out_specs=[HBM] * (1 + ring),
        scratch_shapes=[
            pltpu.VMEM((copies, slots, rhs), BF16),
            pltpu.VMEM((ring, blocks, slots, width), BF16),
            pltpu.SemaphoreType.DMA((1 + ring,)),
        ],
        compiler_params=limit(6),
    )(counts, rounded, deflation, factor)


def halves(value):
    high = value.astype(BF16)
    return high, (value - high.astype(F32)).astype(BF16)


def lower(rows, mine, other):
    sets = len(rows)
    blocks, slots, _ = rows[0].shape
    count, _, rhs = mine.shape
    per = count // blocks

    def body(*refs):
        rows, (mine, other, out) = refs[:sets], refs[sets:]
        first = lax.axis_index("c") == 0
        total = None
        for j in range(blocks):
            pieces = []
            for y in range(per):
                a, b = mine[j * per + y], other[j * per + y]
                pieces += [jnp.where(first, a, b), jnp.where(first, b, a)]
            factor = jnp.concatenate([r[j] for r in rows], 0)
            part = jnp.dot(factor, jnp.concatenate(pieces, 0), preferred_element_type=F32)
            total = part if total is None else total + part
        for n in range(sets):
            out[n] = total[n * slots : (n + 1) * slots]

    return pl.pallas_call(
        body,
        out_shape=struct((sets, slots, rhs), F32),
        in_specs=[VMEM] * (sets + 2),
        out_specs=VMEM,
        compiler_params=limit(8),
    )(*rows, mine, other)


def raise_back(rows, partial, received):
    sets = len(rows)
    blocks, slots, width = rows[0].shape
    rhs = partial.shape[2]
    per = width // (2 * slots)

    def body(*refs):
        rows, partial, received = refs[:sets], refs[sets], refs[sets + 1 : 2 * sets]
        mine, other = refs[2 * sets :]
        first = lax.axis_index("c") == 0
        sums = []
        for n in range(sets):
            total = partial[n]
            for step in range(1, sets):
                total = total + received[step - 1][(n - step) % sets]
            sums.append(total)
        lowered_high, lowered_low = halves(jnp.concatenate(sums, 0))
        over = (((0,), (0,)), ((), ()))
        for j in range(blocks):
            factor = jnp.concatenate([r[j] for r in rows], 0)
            part = lax.dot_general(factor, lowered_high, over, preferred_element_type=F32)
            part = part + lax.dot_general(factor, lowered_low, over, preferred_element_type=F32)
            for y in range(per):
                a = part[2 * y * slots : (2 * y + 1) * slots]
                b = part[(2 * y + 1) * slots : (2 * y + 2) * slots]
                mine[j * per + y] = jnp.where(first, a, b)
                other[j * per + y] = jnp.where(first, b, a).astype(BF16)

    shape = (blocks * per, slots, rhs)
    return pl.pallas_call(
        body,
        out_shape=[struct(shape, F32), struct(shape, BF16)],
        in_specs=[VMEM] * (2 * sets),
        out_specs=[VMEM, VMEM],
        compiler_params=limit(8),
    )(*rows, partial, *received)


def leave(counts, first_level, terms_in, deflation):
    cx, cy, rhs, line = first_level.shape
    slots = deflation.shape[2]

    def body(count, first_level, terms_in, vectors, out, made, sems):
        total = terms_in[0].astype(F32)
        for i in range(1, terms_in.shape[0]):
            total = total + terms_in[i].astype(F32)
        solved = jnp.where(keep_mask(count, slots, rhs), total, 0.0).astype(BF16)
        saves = []
        for a in range(cx):
            for b in range(cy):
                value = lax.dot_general(
                    solved, vectors[a, b], (((0,), (0,)), ((), ())), preferred_element_type=F32
                )
                made[a, b] = value + first_level[a, b]
                saves.append(pltpu.make_async_copy(made.at[a, b], out.at[a, b], sems.at[a, b]))
                saves[-1].start()
        for save in saves:
            save.wait()

    return pl.pallas_call(
        body,
        out_shape=struct(first_level.shape, F32),
        in_specs=[SMEM, VMEM, VMEM, VMEM],
        out_specs=HBM,
        scratch_shapes=[pltpu.VMEM(first_level.shape, F32), pltpu.SemaphoreType.DMA((cx, cy))],
        compiler_params=limit(6),
    )(counts, first_level, terms_in, deflation)


def solution(mesh):
    n_grp, n_sub = mesh.shape["grp"], mesh.shape["sub"]
    sizes = {"zh": 2, "x": n_grp // 2, "zl": 2, "y": n_sub // 4, "c": 2}
    fine = Mesh(mesh.devices.reshape([sizes[a] for a in AXES]), AXES)

    def body(residual_field, line_inverse, deflation, counts, coarse_factor):
        tie = lax.optimization_barrier
        ring = sizes["x"]

        rounded, to_near, to_far = round_cells(residual_field)
        near, far = swap_pairs(to_near, GRP, n_grp, 0), swap_pairs(to_far, GRP, n_grp, 1)
        receivers = sizes["zh"] * sizes["zl"] * sizes["y"]
        spread, *parts = prepare(rounded, deflation, counts, coarse_factor, receivers, ring, sizes["zh"])
        moved = {n: rotate(parts[n], RING, ring, n) for n in (2, 1, 3)}
        rows = [parts[0]] + [moved[n] for n in range(1, ring)]
        far, _ = tie((far, parts[0]))
        to_pair, to_outer, own, ends = columns(near, far, rounded)
        outer, pair = swap_outward(to_outer, n_sub), swap(to_pair, "c")
        spread, _ = tie((spread, to_outer))
        gathered = lax.all_to_all(spread, SPREAD, 0, 0)
        outer, rows[0], rows[2], rows[1], rows[3] = tie((outer, rows[0], rows[2], rows[1], rows[3]))

        to_pair, to_outer, own, ends = rim_lines((own, ends, pair, outer), line_inverse)
        from_outer, from_pair = swap_outward(to_outer, n_sub), swap(to_pair, "c")
        gathered, _ = tie((gathered, to_outer))
        partial = lower(rows, gathered, swap(gathered, "c"))
        received = [rotate(partial, RING, ring, n) for n in range(1, ring)]
        own, _ = tie((own, partial))
        to_near, to_far = row_lines((own, ends, pair, outer), line_inverse, from_pair, from_outer)
        partial, _ = tie((partial, to_near))
        own_terms, other_terms = raise_back(rows, partial, received)
        to_near, to_far, other_terms = tie((to_near, to_far, other_terms))
        from_near, from_far = swap_pairs(to_near, GRP, n_grp, 0), swap_pairs(to_far, GRP, n_grp, 1)
        terms_out = (own_terms + swap(other_terms, "c").astype(F32)).astype(BF16)
        terms_in = lax.all_to_all(terms_out, SPREAD, 0, 0)
        own, _ = tie((own, terms_out))
        inner = inner_lines((own, ends, pair, outer), line_inverse)
        inner, from_far = tie((inner, from_far))
        first_level = collect(inner, from_pair, from_outer, from_near, from_far)
        return leave(counts, first_level, terms_in, deflation)

    return jax.shard_map(
        body,
        mesh=fine,
        in_specs=(
            P(GRP, SUB, None, None),
            P(GRP, SUB, None, None, None),
            P(GRP, SUB, None, None),
            P(GRP, SUB),
            P(AXES, None),
        ),
        out_specs=P(GRP, SUB, None, None),
        check_vma=False,
    )
```

```python
import jax
import jax.numpy as jnp
from jax import lax
from jax.experimental import pallas as pl
from jax.experimental.pallas import tpu as pltpu
from jax.sharding import Mesh, PartitionSpec as P

AXES = ("zh", "x", "zl", "y", "c")
GRP = ("zh", "x")
SUB = ("zl", "y", "c")
SPREAD = ("zh", "zl", "y")
RING = "x"

STEPS = ((-1, 0), (0, -1), (0, 0), (0, 1), (1, 0))
WIDE = 4
VMEM = pl.BlockSpec(memory_space=pltpu.VMEM)
SMEM = pl.BlockSpec(memory_space=pltpu.SMEM)
ANY = pl.BlockSpec(memory_space=pl.ANY)
HBM = pl.BlockSpec(memory_space=pltpu.HBM)
MIB = 1024 * 1024
F32 = jnp.float32
BF16 = jnp.bfloat16


def limit(mib):
    return pltpu.CompilerParams(vmem_limit_bytes=mib * MIB)


def struct(shape, dtype):
    return jax.ShapeDtypeStruct(shape, dtype)


def estimate(flops, size):
    return pl.CostEstimate(flops=flops, bytes_accessed=size, transcendentals=0)


def rotate(value, axes, size, step):
    return lax.ppermute(value, axes, [(i, (i + step) % size) for i in range(size)])


def swap(value, axis):
    return lax.ppermute(value, axis, [(0, 1), (1, 0)])


def swap_pairs(value, axes, size, begin):
    pairs = []
    for i in range(begin, size - 1, 2):
        pairs += [(i, i + 1), (i + 1, i)]
    return lax.ppermute(value, axes, pairs)


def swap_outward(value, size):
    pairs = []
    for i in range(1, size, 2):
        pairs += [(i, (i + 1) % size), ((i + 1) % size, i)]
    return lax.ppermute(value, SUB, pairs)


def present(flag, value):
    return jnp.where(flag, value, jnp.zeros_like(value))


def terms(a, b):
    found = []
    for k, (p, q) in enumerate(STEPS):
        if 0 <= a + p < WIDE and 0 <= b + q < WIDE:
            found.append((k, a + p, b + q))
    return found


def position():
    spot = {axis: lax.axis_index(axis) for axis in AXES}
    size = {axis: lax.axis_size(axis) for axis in AXES}
    core, x = spot["c"], spot["x"]
    before = jnp.logical_or(spot["zh"] > 0, x > 0)
    after = jnp.logical_or(spot["zh"] < size["zh"] - 1, x < size["x"] - 1)
    outward = spot["zl"] * size["y"] + spot["y"]
    past = jnp.where(core == 0, outward > 0, outward < size["zl"] * size["y"] - 1)
    return core, before, after, past, lax.rem(x, 2)


def line_kernel(cells, put, fetch, own, ends, pair, outer, blocks, *rest):
    at = position()
    more, (sides, held, sems) = rest[:-3], rest[-3:]
    if fetch:
        (window_sems, stage, stage_sems), targets, outs = more[-3:], more[-5:-3], more[:-5]
        more = (outs, stage, stage_sems)
        loads = []
        for i, (source, target) in enumerate(zip((own, ends), targets)):
            loads.append(pltpu.make_async_copy(source, target, window_sems.at[i]))
            loads[i].start()
        own, ends = targets
    slot, plan = 0, []
    for a, b in cells:
        found = terms(a, b)
        start, run, copies = slot, 0, []
        for i, (k, _, _) in enumerate(found):
            run += 1
            if i + 1 == len(found) or found[i + 1][0] != k + 1:
                source = blocks.at[a, b, pl.ds(k + 1 - run, run)]
                copies.append(pltpu.make_async_copy(source, held.at[pl.ds(slot, run)], sems.at[slot]))
                copies[-1].start()
                slot, run = slot + run, 0
        plan.append((start, copies, found))

    first = at[0] == 0
    for a in range(WIDE):
        near, far = pair[a, 0], present(at[3], outer[a, 0])
        sides[0, a] = jnp.where(first, far, near)
        sides[1, a] = jnp.where(first, near, far)
    if fetch:
        for load in loads:
            load.wait()

    def window(a, b):
        if b == 0:
            return sides[0, a]
        if b == WIDE - 1:
            return sides[1, a]
        if a in (0, WIDE - 1):
            return ends[0 if a == 0 else 1, b - 1]
        return own[a - 1, b - 1]

    line = held.shape[-1]
    for (a, b), (start, copies, found) in zip(cells, plan):
        for copy in copies:
            copy.wait()
        sources = jnp.concatenate([window(sa, sb) for _, sa, sb in found], axis=1)
        weights = held[start : start + len(found)].reshape(len(found) * line, line)
        put(a, b, jnp.dot(sources, weights, preferred_element_type=F32), at, more)
    if fetch:
        for i in range(2):
            for a in range(WIDE):
                pltpu.make_async_copy(stage.at[i, a], outs[i].at[a, 0], stage_sems.at[i, a]).wait()


def line_solve(cells, put, shapes, windows, line_inverse, extra=(), fetch=False):
    count = sum(len(terms(a, b)) for a, b in cells)
    line = line_inverse.shape[-1]
    rhs = windows[0].shape[2]

    def body(*refs):
        line_kernel(cells, put, fetch, *refs)

    out_specs, scratch = [VMEM] * len(shapes), []
    if fetch:
        shapes = shapes + [struct(w.shape, w.dtype) for w in windows[:2]]
        out_specs = [HBM] * 2 + [VMEM] * 2
        scratch = [
            pltpu.SemaphoreType.DMA((2,)),
            pltpu.VMEM((2, WIDE, rhs, line), BF16),
            pltpu.SemaphoreType.DMA((2, WIDE)),
        ]
    return pl.pallas_call(
        body,
        out_shape=shapes,
        in_specs=[ANY if fetch else VMEM] * 2 + [VMEM] * 2 + [HBM] + [VMEM] * len(extra),
        out_specs=out_specs,
        scratch_shapes=scratch
        + [
            pltpu.VMEM((2, WIDE, rhs, line), BF16),
            pltpu.VMEM((count, line, line), line_inverse.dtype),
            pltpu.SemaphoreType.DMA((count,)),
        ],
        compiler_params=limit(42),
        cost_estimate=estimate(2 * count * rhs * line * line, count * line * line * 2),
    )(*windows, line_inverse, *extra)


def put_rim(a, b, value, at, refs):
    outs, stage, sems = refs
    value = value.astype(BF16)
    first = at[0] == 0
    to_pair = first if b else jnp.logical_not(first)
    for i, chosen in ((0, to_pair), (1, jnp.logical_not(to_pair))):

        @pl.when(chosen)
        def _(i=i):
            stage[i, a] = value
            pltpu.make_async_copy(stage.at[i, a], outs[i].at[a, 0], sems.at[i, a]).start()


def returned(at, from_pair, from_outer, a, b):
    near, far = from_pair[a, 0], present(at[3], from_outer[a, 0])
    return jnp.where((at[0] == 0) == (b == 1), far, near).astype(F32)


def put_rows(a, b, value, at, refs):
    from_pair, from_outer, near, far = refs
    value = (value + returned(at, from_pair, from_outer, a, b)).astype(BF16)
    to_near = (at[4] == 0) == (a != 0)

    @pl.when(to_near)
    def _():
        near[0, b - 1] = value

    @pl.when(jnp.logical_not(to_near))
    def _():
        far[0, b - 1] = value


def put_inner(a, b, value, at, refs):
    refs[-1][a - 1, b - 1] = value


def columns(near, far, rounded):
    rhs, line = rounded.shape[2:]

    def body(near, far, rounded, pair, outer, own, ends):
        at = position()
        first, even = at[0] == 0, at[4] == 0
        for a in range(WIDE):
            if a in (0, WIDE - 1):
                for b in range(2):
                    low, high = (far, near) if a == 0 else (near, far)
                    ends[a // 2, b] = present(at[1 + a // 2], jnp.where(even, low[0, b], high[0, b]))
                left, right = ends[a // 2, 0], ends[a // 2, 1]
            else:
                left, right = rounded[a - 1, 0], rounded[a - 1, 1]
                own[a - 1, 0], own[a - 1, 1] = left, right
            pair[a, 0] = jnp.where(first, right, left)
            outer[a, 0] = jnp.where(first, left, right)

    out, square = struct((WIDE, 1, rhs, line), BF16), struct(rounded.shape, BF16)
    return pl.pallas_call(
        body,
        out_shape=[out, out, square, square],
        in_specs=[VMEM] * 3,
        out_specs=[VMEM] * 4,
        compiler_params=limit(4),
    )(near, far, rounded)


def rim_lines(windows, line_inverse):
    _, _, rhs, line = windows[0].shape
    column = struct((WIDE, 1, rhs, line), BF16)
    cells = [(a, b) for a in range(WIDE) for b in (0, WIDE - 1)]
    return line_solve(cells, put_rim, [column, column], windows, line_inverse, fetch=True)


def row_lines(windows, line_inverse, from_pair, from_outer):
    _, _, rhs, line = windows[0].shape
    row = struct((1, 2, rhs, line), BF16)
    cells = [(a, b) for a in (0, WIDE - 1) for b in (1, 2)]
    return line_solve(cells, put_rows, [row, row], windows, line_inverse, (from_pair, from_outer))


def inner_lines(windows, line_inverse):
    cells = [(a, b) for a in (1, 2) for b in (1, 2)]
    return line_solve(cells, put_inner, [struct(windows[0].shape, F32)], windows, line_inverse)[0]


def collect(inner, from_pair, from_outer, from_near, from_far):
    cx, cy, _, _ = inner.shape

    def body(inner, from_pair, from_outer, from_near, from_far, out):
        at = position()
        for a in range(cx):
            for b in range(cy):
                side = returned(at, from_pair, from_outer, a + 1, b + 1)
                low, high = (from_far, from_near) if a == 0 else (from_near, from_far)
                across = present(at[1 + a], jnp.where(at[4] == 0, low[0, b], high[0, b])).astype(F32)
                out[a, b] = inner[a, b] + side + across

    return pl.pallas_call(
        body,
        out_shape=struct(inner.shape, F32),
        in_specs=[VMEM] * 5,
        out_specs=VMEM,
        compiler_params=limit(8),
        cost_estimate=estimate(10**9, 4 * 10**6),
    )(inner, from_pair, from_outer, from_near, from_far)


def keep_mask(count, slots, rhs):
    return lax.broadcasted_iota(jnp.int32, (slots, rhs), 0) < count[0, 0]


def round_cells(residual_field):
    cx, cy, rhs, line = residual_field.shape

    def body(residual, rounded, near, far):
        even = position()[4] == 0
        for b in range(cy):
            first, second = residual[0, b].astype(BF16), residual[1, b].astype(BF16)
            rounded[0, b], rounded[1, b] = first, second
            near[0, b] = jnp.where(even, second, first)
            far[0, b] = jnp.where(even, first, second)

    row = struct((1, cy, rhs, line), BF16)
    return pl.pallas_call(
        body,
        out_shape=[struct(residual_field.shape, BF16), row, row],
        in_specs=[VMEM],
        out_specs=[VMEM] * 3,
        compiler_params=limit(4),
    )(residual_field)


def prepare(rounded, deflation, counts, factor, copies, ring, blocks):
    slots, line = deflation.shape[2:]
    cx, cy, rhs, _ = rounded.shape
    width = factor.shape[1] // (ring * blocks)

    def body(count, rounded, vectors, factor, *refs):
        spread, parts = refs[0], refs[1 : 1 + ring]
        made, cut, sems = refs[1 + ring :]
        here = lax.axis_index("x")
        saves = []
        for step in range(ring):
            n = (step + 1) % ring
            there = lax.rem(here + n, ring)
            for j in range(blocks):
                start = pl.multiple_of((j * ring + there) * width, width)
                cut[n, j] = factor[:, pl.ds(start, width)]
            saves.append(pltpu.make_async_copy(cut.at[n], parts[n], sems.at[n]))
            saves[-1].start()
        total = None
        for a in range(cx):
            for b in range(cy):
                part = lax.dot_general(
                    vectors[a, b], rounded[a, b], (((1,), (1,)), ((), ())), preferred_element_type=F32
                )
                total = part if total is None else total + part
        total = jnp.where(keep_mask(count, slots, rhs), total, 0.0)
        for i in range(copies):
            made[i] = total
        saves.append(pltpu.make_async_copy(made, spread, sems.at[ring]))
        saves[-1].start()
        for save in saves:
            save.wait()

    return pl.pallas_call(
        body,
        out_shape=[struct((copies, slots, rhs), F32)] + [struct((blocks, slots, width), F32)] * ring,
        in_specs=[SMEM, VMEM, VMEM, VMEM],
        out_specs=[HBM] * (1 + ring),
        scratch_shapes=[
            pltpu.VMEM((copies, slots, rhs), F32),
            pltpu.VMEM((ring, blocks, slots, width), F32),
            pltpu.SemaphoreType.DMA((1 + ring,)),
        ],
        compiler_params=limit(8),
    )(counts, rounded, deflation, factor)


def halves(value):
    high = value.astype(BF16)
    return high, (value - high.astype(F32)).astype(BF16)


def lower(rows, mine, other):
    sets = len(rows)
    blocks, slots, _ = rows[0].shape
    count, _, rhs = mine.shape
    per = count // blocks

    def body(*refs):
        rows, (mine, other, out) = refs[:sets], refs[sets:]
        first = lax.axis_index("c") == 0
        total = None
        for j in range(blocks):
            pieces = []
            for y in range(per):
                a, b = mine[j * per + y], other[j * per + y]
                pieces += [jnp.where(first, a, b), jnp.where(first, b, a)]
            high, low = halves(jnp.concatenate([r[j] for r in rows], 0))
            vector_high, vector_low = halves(jnp.concatenate(pieces, 0))
            part = jnp.dot(high, vector_high, preferred_element_type=F32)
            part = part + jnp.dot(high, vector_low, preferred_element_type=F32)
            part = part + jnp.dot(low, vector_high, preferred_element_type=F32)
            total = part if total is None else total + part
        for n in range(sets):
            out[n] = total[n * slots : (n + 1) * slots]

    return pl.pallas_call(
        body,
        out_shape=struct((sets, slots, rhs), F32),
        in_specs=[VMEM] * (sets + 2),
        out_specs=VMEM,
        compiler_params=limit(8),
    )(*rows, mine, other)


def raise_back(rows, partial, received):
    sets = len(rows)
    blocks, slots, width = rows[0].shape
    rhs = partial.shape[2]
    per = width // (2 * slots)

    def body(*refs):
        rows, partial, received = refs[:sets], refs[sets], refs[sets + 1 : 2 * sets]
        mine, other = refs[2 * sets :]
        first = lax.axis_index("c") == 0
        sums = []
        for n in range(sets):
            total = partial[n]
            for step in range(1, sets):
                total = total + received[step - 1][(n - step) % sets]
            sums.append(total)
        lowered_high, lowered_low = halves(jnp.concatenate(sums, 0))
        over = (((0,), (0,)), ((), ()))
        for j in range(blocks):
            high, low = halves(jnp.concatenate([r[j] for r in rows], 0))
            part = lax.dot_general(high, lowered_high, over, preferred_element_type=F32)
            part = part + lax.dot_general(high, lowered_low, over, preferred_element_type=F32)
            part = part + lax.dot_general(low, lowered_high, over, preferred_element_type=F32)
            for y in range(per):
                a = part[2 * y * slots : (2 * y + 1) * slots]
                b = part[(2 * y + 1) * slots : (2 * y + 2) * slots]
                mine[j * per + y] = jnp.where(first, a, b)
                other[j * per + y] = jnp.where(first, b, a)

    shape = (blocks * per, slots, rhs)
    return pl.pallas_call(
        body,
        out_shape=[struct(shape, F32)] * 2,
        in_specs=[VMEM] * (2 * sets),
        out_specs=[VMEM, VMEM],
        compiler_params=limit(8),
    )(*rows, partial, *received)


def leave(counts, first_level, terms_in, deflation):
    cx, cy, rhs, line = first_level.shape
    slots = deflation.shape[2]

    def body(count, first_level, terms_in, vectors, out, made, sems):
        total = terms_in[0].astype(F32)
        for i in range(1, terms_in.shape[0]):
            total = total + terms_in[i].astype(F32)
        solved = jnp.where(keep_mask(count, slots, rhs), total, 0.0).astype(BF16)
        saves = []
        for a in range(cx):
            for b in range(cy):
                value = lax.dot_general(
                    solved, vectors[a, b], (((0,), (0,)), ((), ())), preferred_element_type=F32
                )
                made[a, b] = value + first_level[a, b]
                saves.append(pltpu.make_async_copy(made.at[a, b], out.at[a, b], sems.at[a, b]))
                saves[-1].start()
        for save in saves:
            save.wait()

    return pl.pallas_call(
        body,
        out_shape=struct(first_level.shape, F32),
        in_specs=[SMEM, VMEM, VMEM, VMEM],
        out_specs=HBM,
        scratch_shapes=[pltpu.VMEM(first_level.shape, F32), pltpu.SemaphoreType.DMA((cx, cy))],
        compiler_params=limit(6),
    )(counts, first_level, terms_in, deflation)


def solution(mesh):
    n_grp, n_sub = mesh.shape["grp"], mesh.shape["sub"]
    sizes = {"zh": 2, "x": n_grp // 2, "zl": 2, "y": n_sub // 4, "c": 2}
    fine = Mesh(mesh.devices.reshape([sizes[a] for a in AXES]), AXES)

    def body(residual_field, line_inverse, deflation, counts, coarse_factor):
        tie = lax.optimization_barrier
        ring = sizes["x"]

        rounded, to_near, to_far = round_cells(residual_field)
        near, far = swap_pairs(to_near, GRP, n_grp, 0), swap_pairs(to_far, GRP, n_grp, 1)
        receivers = sizes["zh"] * sizes["zl"] * sizes["y"]
        spread, *parts = prepare(rounded, deflation, counts, coarse_factor, receivers, ring, sizes["zh"])
        moved = {n: rotate(parts[n], RING, ring, n) for n in (2, 1, 3)}
        rows = [parts[0]] + [moved[n] for n in range(1, ring)]
        far, _ = tie((far, parts[0]))
        to_pair, to_outer, own, ends = columns(near, far, rounded)
        outer, pair = swap_outward(to_outer, n_sub), swap(to_pair, "c")
        spread, _ = tie((spread, to_outer))
        gathered = lax.all_to_all(spread, SPREAD, 0, 0)
        outer, rows[0], rows[2], rows[1], rows[3] = tie((outer, rows[0], rows[2], rows[1], rows[3]))

        to_pair, to_outer, own, ends = rim_lines((own, ends, pair, outer), line_inverse)
        from_outer, from_pair = swap_outward(to_outer, n_sub), swap(to_pair, "c")
        gathered, _ = tie((gathered, to_outer))
        partial = lower(rows, gathered, swap(gathered, "c"))
        moved = {n: rotate(partial, RING, ring, n) for n in (2, 1, 3)}
        received = [moved[n] for n in range(1, ring)]
        own, _ = tie((own, partial))
        to_near, to_far = row_lines((own, ends, pair, outer), line_inverse, from_pair, from_outer)
        partial, received[1], received[0], received[2], _ = tie((partial, received[1], received[0], received[2], to_near))
        own_terms, other_terms = raise_back(rows, partial, received)
        to_near, to_far, other_terms = tie((to_near, to_far, other_terms))
        from_near, from_far = swap_pairs(to_near, GRP, n_grp, 0), swap_pairs(to_far, GRP, n_grp, 1)
        terms_out = own_terms + swap(other_terms, "c")
        terms_in = lax.all_to_all(terms_out, SPREAD, 0, 0)
        own, _ = tie((own, terms_out))
        inner = inner_lines((own, ends, pair, outer), line_inverse)
        inner, from_far = tie((inner, from_far))
        first_level = collect(inner, from_pair, from_outer, from_near, from_far)
        return leave(counts, first_level, terms_in, deflation)

    return jax.shard_map(
        body,
        mesh=fine,
        in_specs=(
            P(GRP, SUB, None, None),
            P(GRP, SUB, None, None, None),
            P(GRP, SUB, None, None),
            P(GRP, SUB),
            P(AXES, None),
        ),
        out_specs=P(GRP, SUB, None, None),
        check_vma=False,
    )
```

```python
import jax
import jax.numpy as jnp
from jax import lax
from jax.experimental import pallas as pl
from jax.experimental.pallas import tpu as pltpu
from jax.sharding import Mesh, PartitionSpec as P

AXES = ("zh", "x", "zl", "y", "c")
GRP = ("zh", "x")
SUB = ("zl", "y", "c")
SPREAD = ("zh", "zl", "y")
RING = "x"

STEPS = ((-1, 0), (0, -1), (0, 0), (0, 1), (1, 0))
WIDE = 4
VMEM = pl.BlockSpec(memory_space=pltpu.VMEM)
SMEM = pl.BlockSpec(memory_space=pltpu.SMEM)
ANY = pl.BlockSpec(memory_space=pl.ANY)
HBM = pl.BlockSpec(memory_space=pltpu.HBM)
MIB = 1024 * 1024
F32 = jnp.float32
BF16 = jnp.bfloat16


def limit(mib):
    return pltpu.CompilerParams(vmem_limit_bytes=mib * MIB)


def struct(shape, dtype):
    return jax.ShapeDtypeStruct(shape, dtype)


def estimate(flops, size):
    return pl.CostEstimate(flops=flops, bytes_accessed=size, transcendentals=0)


def rotate(value, axes, size, step):
    return lax.ppermute(value, axes, [(i, (i + step) % size) for i in range(size)])


def swap(value, axis):
    return lax.ppermute(value, axis, [(0, 1), (1, 0)])


def swap_pairs(value, axes, size, begin):
    pairs = []
    for i in range(begin, size - 1, 2):
        pairs += [(i, i + 1), (i + 1, i)]
    return lax.ppermute(value, axes, pairs)


def swap_outward(value, size):
    pairs = []
    for i in range(1, size, 2):
        pairs += [(i, (i + 1) % size), ((i + 1) % size, i)]
    return lax.ppermute(value, SUB, pairs)


def present(flag, value):
    return jnp.where(flag, value, jnp.zeros_like(value))


def terms(a, b):
    found = []
    for k, (p, q) in enumerate(STEPS):
        if 0 <= a + p < WIDE and 0 <= b + q < WIDE:
            found.append((k, a + p, b + q))
    return found


def position():
    spot = {axis: lax.axis_index(axis) for axis in AXES}
    size = {axis: lax.axis_size(axis) for axis in AXES}
    core, x = spot["c"], spot["x"]
    before = jnp.logical_or(spot["zh"] > 0, x > 0)
    after = jnp.logical_or(spot["zh"] < size["zh"] - 1, x < size["x"] - 1)
    outward = spot["zl"] * size["y"] + spot["y"]
    past = jnp.where(core == 0, outward > 0, outward < size["zl"] * size["y"] - 1)
    return core, before, after, past, lax.rem(x, 2)


def line_kernel(cells, put, fetch, own, ends, pair, outer, blocks, *rest):
    at = position()
    more, (sides, held, sems) = rest[:-3], rest[-3:]
    if fetch:
        (window_sems, stage, stage_sems), targets, outs = more[-3:], more[-5:-3], more[:-5]
        more = (outs, stage, stage_sems)
        loads = []
        for i, (source, target) in enumerate(zip((own, ends), targets)):
            loads.append(pltpu.make_async_copy(source, target, window_sems.at[i]))
            loads[i].start()
        own, ends = targets
    slot, plan = 0, []
    for a, b in cells:
        found = terms(a, b)
        start, run, copies = slot, 0, []
        for i, (k, _, _) in enumerate(found):
            run += 1
            if i + 1 == len(found) or found[i + 1][0] != k + 1:
                source = blocks.at[a, b, pl.ds(k + 1 - run, run)]
                copies.append(pltpu.make_async_copy(source, held.at[pl.ds(slot, run)], sems.at[slot]))
                copies[-1].start()
                slot, run = slot + run, 0
        plan.append((start, copies, found))

    first = at[0] == 0
    for a in range(WIDE):
        near, far = pair[a, 0], present(at[3], outer[a, 0])
        sides[0, a] = jnp.where(first, far, near)
        sides[1, a] = jnp.where(first, near, far)
    if fetch:
        for load in loads:
            load.wait()

    def window(a, b):
        if b == 0:
            return sides[0, a]
        if b == WIDE - 1:
            return sides[1, a]
        if a in (0, WIDE - 1):
            return ends[0 if a == 0 else 1, b - 1]
        return own[a - 1, b - 1]

    line = held.shape[-1]
    for (a, b), (start, copies, found) in zip(cells, plan):
        for copy in copies:
            copy.wait()
        sources = jnp.concatenate([window(sa, sb) for _, sa, sb in found], axis=1)
        weights = held[start : start + len(found)].reshape(len(found) * line, line)
        put(a, b, jnp.dot(sources, weights, preferred_element_type=F32), at, more)
    if fetch:
        for i in range(2):
            for a in range(WIDE):
                pltpu.make_async_copy(stage.at[i, a], outs[i].at[a, 0], stage_sems.at[i, a]).wait()


def line_solve(cells, put, shapes, windows, line_inverse, extra=(), fetch=False):
    count = sum(len(terms(a, b)) for a, b in cells)
    line = line_inverse.shape[-1]
    rhs = windows[0].shape[2]

    def body(*refs):
        line_kernel(cells, put, fetch, *refs)

    out_specs, scratch = [VMEM] * len(shapes), []
    if fetch:
        shapes = shapes + [struct(w.shape, w.dtype) for w in windows[:2]]
        out_specs = [HBM] * 2 + [VMEM] * 2
        scratch = [
            pltpu.SemaphoreType.DMA((2,)),
            pltpu.VMEM((2, WIDE, rhs, line), BF16),
            pltpu.SemaphoreType.DMA((2, WIDE)),
        ]
    return pl.pallas_call(
        body,
        out_shape=shapes,
        in_specs=[ANY if fetch else VMEM] * 2 + [VMEM] * 2 + [HBM] + [VMEM] * len(extra),
        out_specs=out_specs,
        scratch_shapes=scratch
        + [
            pltpu.VMEM((2, WIDE, rhs, line), BF16),
            pltpu.VMEM((count, line, line), line_inverse.dtype),
            pltpu.SemaphoreType.DMA((count,)),
        ],
        compiler_params=limit(42),
        cost_estimate=estimate(2 * count * rhs * line * line, count * line * line * 2),
    )(*windows, line_inverse, *extra)


def put_rim(a, b, value, at, refs):
    outs, stage, sems = refs
    value = value.astype(BF16)
    first = at[0] == 0
    to_pair = first if b else jnp.logical_not(first)
    for i, chosen in ((0, to_pair), (1, jnp.logical_not(to_pair))):

        @pl.when(chosen)
        def _(i=i):
            stage[i, a] = value
            pltpu.make_async_copy(stage.at[i, a], outs[i].at[a, 0], sems.at[i, a]).start()


def returned(at, from_pair, from_outer, a, b):
    near, far = from_pair[a, 0], present(at[3], from_outer[a, 0])
    return jnp.where((at[0] == 0) == (b == 1), far, near).astype(F32)


def put_rows(a, b, value, at, refs):
    from_pair, from_outer, near, far = refs
    value = (value + returned(at, from_pair, from_outer, a, b)).astype(BF16)
    to_near = (at[4] == 0) == (a != 0)

    @pl.when(to_near)
    def _():
        near[0, b - 1] = value

    @pl.when(jnp.logical_not(to_near))
    def _():
        far[0, b - 1] = value


def put_inner(a, b, value, at, refs):
    refs[-1][a - 1, b - 1] = value


def columns(near, far, rounded):
    rhs, line = rounded.shape[2:]

    def body(near, far, rounded, pair, outer, own, ends):
        at = position()
        first, even = at[0] == 0, at[4] == 0
        for a in range(WIDE):
            if a in (0, WIDE - 1):
                for b in range(2):
                    low, high = (far, near) if a == 0 else (near, far)
                    ends[a // 2, b] = present(at[1 + a // 2], jnp.where(even, low[0, b], high[0, b]))
                left, right = ends[a // 2, 0], ends[a // 2, 1]
            else:
                left, right = rounded[a - 1, 0], rounded[a - 1, 1]
                own[a - 1, 0], own[a - 1, 1] = left, right
            pair[a, 0] = jnp.where(first, right, left)
            outer[a, 0] = jnp.where(first, left, right)

    out, square = struct((WIDE, 1, rhs, line), BF16), struct(rounded.shape, BF16)
    return pl.pallas_call(
        body,
        out_shape=[out, out, square, square],
        in_specs=[VMEM] * 3,
        out_specs=[VMEM] * 4,
        compiler_params=limit(4),
    )(near, far, rounded)


def rim_lines(windows, line_inverse):
    _, _, rhs, line = windows[0].shape
    column = struct((WIDE, 1, rhs, line), BF16)
    cells = [(a, b) for a in range(WIDE) for b in (0, WIDE - 1)]
    return line_solve(cells, put_rim, [column, column], windows, line_inverse, fetch=True)


def row_lines(windows, line_inverse, from_pair, from_outer):
    _, _, rhs, line = windows[0].shape
    row = struct((1, 2, rhs, line), BF16)
    cells = [(a, b) for a in (0, WIDE - 1) for b in (1, 2)]
    return line_solve(cells, put_rows, [row, row], windows, line_inverse, (from_pair, from_outer))


def inner_lines(windows, line_inverse):
    cells = [(a, b) for a in (1, 2) for b in (1, 2)]
    return line_solve(cells, put_inner, [struct(windows[0].shape, F32)], windows, line_inverse)[0]


def collect(inner, from_pair, from_outer, from_near, from_far):
    cx, cy, _, _ = inner.shape

    def body(inner, from_pair, from_outer, from_near, from_far, out):
        at = position()
        for a in range(cx):
            for b in range(cy):
                side = returned(at, from_pair, from_outer, a + 1, b + 1)
                low, high = (from_far, from_near) if a == 0 else (from_near, from_far)
                across = present(at[1 + a], jnp.where(at[4] == 0, low[0, b], high[0, b])).astype(F32)
                out[a, b] = inner[a, b] + side + across

    return pl.pallas_call(
        body,
        out_shape=struct(inner.shape, F32),
        in_specs=[VMEM] * 5,
        out_specs=VMEM,
        compiler_params=limit(8),
        cost_estimate=estimate(10**9, 4 * 10**6),
    )(inner, from_pair, from_outer, from_near, from_far)


def keep_mask(count, slots, rhs):
    return lax.broadcasted_iota(jnp.int32, (slots, rhs), 0) < count[0, 0]


def round_cells(residual_field):
    cx, cy, rhs, line = residual_field.shape

    def body(residual, rounded, near, far):
        even = position()[4] == 0
        for b in range(cy):
            first, second = residual[0, b].astype(BF16), residual[1, b].astype(BF16)
            rounded[0, b], rounded[1, b] = first, second
            near[0, b] = jnp.where(even, second, first)
            far[0, b] = jnp.where(even, first, second)

    row = struct((1, cy, rhs, line), BF16)
    return pl.pallas_call(
        body,
        out_shape=[struct(residual_field.shape, BF16), row, row],
        in_specs=[VMEM],
        out_specs=[VMEM] * 3,
        compiler_params=limit(4),
    )(residual_field)


def prepare(rounded, deflation, counts, factor, copies, ring, blocks):
    slots, line = deflation.shape[2:]
    cx, cy, rhs, _ = rounded.shape
    width = factor.shape[1] // (ring * blocks)

    def body(count, rounded, vectors, factor, *refs):
        spread, parts = refs[0], refs[1 : 1 + ring]
        made, cut, sems = refs[1 + ring :]
        here = lax.axis_index("x")
        saves = []
        for step in range(ring):
            n = (step + 1) % ring
            there = lax.rem(here + n, ring)
            for j in range(blocks):
                start = pl.multiple_of((j * ring + there) * width, width)
                cut[n, j] = factor[:, pl.ds(start, width)].astype(BF16)
            saves.append(pltpu.make_async_copy(cut.at[n], parts[n], sems.at[n]))
            saves[-1].start()
        total = None
        for a in range(cx):
            for b in range(cy):
                part = lax.dot_general(
                    vectors[a, b], rounded[a, b], (((1,), (1,)), ((), ())), preferred_element_type=F32
                )
                total = part if total is None else total + part
        total = jnp.where(keep_mask(count, slots, rhs), total, 0.0).astype(BF16)
        for i in range(copies):
            made[i] = total
        saves.append(pltpu.make_async_copy(made, spread, sems.at[ring]))
        saves[-1].start()
        for save in saves:
            save.wait()

    return pl.pallas_call(
        body,
        out_shape=[struct((copies, slots, rhs), BF16)] + [struct((blocks, slots, width), BF16)] * ring,
        in_specs=[SMEM, VMEM, VMEM, VMEM],
        out_specs=[HBM] * (1 + ring),
        scratch_shapes=[
            pltpu.VMEM((copies, slots, rhs), BF16),
            pltpu.VMEM((ring, blocks, slots, width), BF16),
            pltpu.SemaphoreType.DMA((1 + ring,)),
        ],
        compiler_params=limit(6),
    )(counts, rounded, deflation, factor)


def halves(value):
    high = value.astype(BF16)
    return high, (value - high.astype(F32)).astype(BF16)


def lower(rows, mine, other):
    sets = len(rows)
    blocks, slots, _ = rows[0].shape
    count, _, rhs = mine.shape
    per = count // blocks

    def body(*refs):
        rows, (mine, other, out) = refs[:sets], refs[sets:]
        first = lax.axis_index("c") == 0
        total = None
        for j in range(blocks):
            pieces = []
            for y in range(per):
                a, b = mine[j * per + y], other[j * per + y]
                pieces += [jnp.where(first, a, b), jnp.where(first, b, a)]
            factor = jnp.concatenate([r[j] for r in rows], 0)
            part = jnp.dot(factor, jnp.concatenate(pieces, 0), preferred_element_type=F32)
            total = part if total is None else total + part
        for n in range(sets):
            out[n] = total[n * slots : (n + 1) * slots]

    return pl.pallas_call(
        body,
        out_shape=struct((sets, slots, rhs), F32),
        in_specs=[VMEM] * (sets + 2),
        out_specs=VMEM,
        compiler_params=limit(8),
    )(*rows, mine, other)


def raise_back(rows, partial, received):
    sets = len(rows)
    blocks, slots, width = rows[0].shape
    rhs = partial.shape[2]
    per = width // (2 * slots)

    def body(*refs):
        rows, partial, received = refs[:sets], refs[sets], refs[sets + 1 : 2 * sets]
        mine, other = refs[2 * sets :]
        first = lax.axis_index("c") == 0
        sums = []
        for n in range(sets):
            total = partial[n]
            for step in range(1, sets):
                total = total + received[step - 1][(n - step) % sets]
            sums.append(total)
        lowered_high, lowered_low = halves(jnp.concatenate(sums, 0))
        over = (((0,), (0,)), ((), ()))
        for j in range(blocks):
            factor = jnp.concatenate([r[j] for r in rows], 0)
            part = lax.dot_general(factor, lowered_high, over, preferred_element_type=F32)
            part = part + lax.dot_general(factor, lowered_low, over, preferred_element_type=F32)
            for y in range(per):
                a = part[2 * y * slots : (2 * y + 1) * slots]
                b = part[(2 * y + 1) * slots : (2 * y + 2) * slots]
                mine[j * per + y] = jnp.where(first, a, b)
                other[j * per + y] = jnp.where(first, b, a).astype(BF16)

    shape = (blocks * per, slots, rhs)
    return pl.pallas_call(
        body,
        out_shape=[struct(shape, F32), struct(shape, BF16)],
        in_specs=[VMEM] * (2 * sets),
        out_specs=[VMEM, VMEM],
        compiler_params=limit(8),
    )(*rows, partial, *received)


def leave(counts, first_level, terms_in, deflation):
    cx, cy, rhs, line = first_level.shape
    slots = deflation.shape[2]

    def body(count, first_level, terms_in, vectors, out, made, sems):
        total = terms_in[0].astype(F32)
        for i in range(1, terms_in.shape[0]):
            total = total + terms_in[i].astype(F32)
        solved = jnp.where(keep_mask(count, slots, rhs), total, 0.0).astype(BF16)
        saves = []
        for a in range(cx):
            for b in range(cy):
                value = lax.dot_general(
                    solved, vectors[a, b], (((0,), (0,)), ((), ())), preferred_element_type=F32
                )
                made[a, b] = value + first_level[a, b]
                saves.append(pltpu.make_async_copy(made.at[a, b], out.at[a, b], sems.at[a, b]))
                saves[-1].start()
        for save in saves:
            save.wait()

    return pl.pallas_call(
        body,
        out_shape=struct(first_level.shape, F32),
        in_specs=[SMEM, VMEM, VMEM, VMEM],
        out_specs=HBM,
        scratch_shapes=[pltpu.VMEM(first_level.shape, F32), pltpu.SemaphoreType.DMA((cx, cy))],
        compiler_params=limit(6),
    )(counts, first_level, terms_in, deflation)


def solution(mesh):
    n_grp, n_sub = mesh.shape["grp"], mesh.shape["sub"]
    sizes = {"zh": 2, "x": n_grp // 2, "zl": 2, "y": n_sub // 4, "c": 2}
    fine = Mesh(mesh.devices.reshape([sizes[a] for a in AXES]), AXES)

    def body(residual_field, line_inverse, deflation, counts, coarse_factor):
        tie = lax.optimization_barrier
        ring = sizes["x"]

        rounded, to_near, to_far = round_cells(residual_field)
        near, far = swap_pairs(to_near, GRP, n_grp, 0), swap_pairs(to_far, GRP, n_grp, 1)
        receivers = sizes["zh"] * sizes["zl"] * sizes["y"]
        spread, *parts = prepare(rounded, deflation, counts, coarse_factor, receivers, ring, sizes["zh"])
        moved = {n: rotate(parts[n], RING, ring, n) for n in (2, 1, 3)}
        rows = [parts[0]] + [moved[n] for n in range(1, ring)]
        far, _ = tie((far, parts[0]))
        to_pair, to_outer, own, ends = columns(near, far, rounded)
        outer, pair = swap_outward(to_outer, n_sub), swap(to_pair, "c")
        spread, _ = tie((spread, to_outer))
        gathered = lax.all_to_all(spread, SPREAD, 0, 0)
        outer, rows[0], rows[2], rows[1], rows[3] = tie((outer, rows[0], rows[2], rows[1], rows[3]))

        to_pair, to_outer, own, ends = rim_lines((own, ends, pair, outer), line_inverse)
        from_outer, from_pair = swap_outward(to_outer, n_sub), swap(to_pair, "c")
        gathered, _ = tie((gathered, to_outer))
        partial = lower(rows, gathered, swap(gathered, "c"))
        moved = {n: rotate(partial, RING, ring, n) for n in (2, 1, 3)}
        received = [moved[n] for n in range(1, ring)]
        own, _ = tie((own, partial))
        to_near, to_far = row_lines((own, ends, pair, outer), line_inverse, from_pair, from_outer)
        partial, received[1], received[0], received[2], _ = tie((partial, received[1], received[0], received[2], to_near))
        own_terms, other_terms = raise_back(rows, partial, received)
        to_near, to_far, other_terms = tie((to_near, to_far, other_terms))
        from_near, from_far = swap_pairs(to_near, GRP, n_grp, 0), swap_pairs(to_far, GRP, n_grp, 1)
        terms_out = (own_terms + swap(other_terms, "c").astype(F32)).astype(BF16)
        terms_in = lax.all_to_all(terms_out, SPREAD, 0, 0)
        own, _ = tie((own, terms_out))
        inner = inner_lines((own, ends, pair, outer), line_inverse)
        inner, from_far = tie((inner, from_far))
        first_level = collect(inner, from_pair, from_outer, from_near, from_far)
        return leave(counts, first_level, terms_in, deflation)

    return jax.shard_map(
        body,
        mesh=fine,
        in_specs=(
            P(GRP, SUB, None, None),
            P(GRP, SUB, None, None, None),
            P(GRP, SUB, None, None),
            P(GRP, SUB),
            P(AXES, None),
        ),
        out_specs=P(GRP, SUB, None, None),
        check_vma=False,
    )
```

```python
import jax
import jax.numpy as jnp
from jax import lax
from jax.experimental import pallas as pl
from jax.experimental.pallas import tpu as pltpu
from jax.sharding import Mesh, PartitionSpec as P

AXES = ("zh", "x", "zl", "y", "c")
GRP = ("zh", "x")
SUB = ("zl", "y", "c")
SPREAD = ("zh", "zl", "y")
RING = "x"

STEPS = ((-1, 0), (0, -1), (0, 0), (0, 1), (1, 0))
WIDE = 4
VMEM = pl.BlockSpec(memory_space=pltpu.VMEM)
SMEM = pl.BlockSpec(memory_space=pltpu.SMEM)
ANY = pl.BlockSpec(memory_space=pl.ANY)
HBM = pl.BlockSpec(memory_space=pltpu.HBM)
MIB = 1024 * 1024
F32 = jnp.float32
BF16 = jnp.bfloat16


def limit(mib):
    return pltpu.CompilerParams(vmem_limit_bytes=mib * MIB)


def struct(shape, dtype):
    return jax.ShapeDtypeStruct(shape, dtype)


def estimate(flops, size):
    return pl.CostEstimate(flops=flops, bytes_accessed=size, transcendentals=0)


def rotate(value, axes, size, step):
    return lax.ppermute(value, axes, [(i, (i + step) % size) for i in range(size)])


def swap(value, axis):
    return lax.ppermute(value, axis, [(0, 1), (1, 0)])


def swap_pairs(value, axes, size, begin):
    pairs = []
    for i in range(begin, size - 1, 2):
        pairs += [(i, i + 1), (i + 1, i)]
    return lax.ppermute(value, axes, pairs)


def swap_outward(value, size):
    pairs = []
    for i in range(1, size, 2):
        pairs += [(i, (i + 1) % size), ((i + 1) % size, i)]
    return lax.ppermute(value, SUB, pairs)


def present(flag, value):
    return jnp.where(flag, value, jnp.zeros_like(value))


def terms(a, b):
    found = []
    for k, (p, q) in enumerate(STEPS):
        if 0 <= a + p < WIDE and 0 <= b + q < WIDE:
            found.append((k, a + p, b + q))
    return found


def position():
    spot = {axis: lax.axis_index(axis) for axis in AXES}
    size = {axis: lax.axis_size(axis) for axis in AXES}
    core, x = spot["c"], spot["x"]
    before = jnp.logical_or(spot["zh"] > 0, x > 0)
    after = jnp.logical_or(spot["zh"] < size["zh"] - 1, x < size["x"] - 1)
    outward = spot["zl"] * size["y"] + spot["y"]
    past = jnp.where(core == 0, outward > 0, outward < size["zl"] * size["y"] - 1)
    return core, before, after, past, lax.rem(x, 2)


def line_kernel(cells, put, fetch, own, ends, pair, outer, blocks, *rest):
    at = position()
    more, (sides, held, sems) = rest[:-3], rest[-3:]
    if fetch:
        (window_sems, stage, stage_sems), targets, outs = more[-3:], more[-5:-3], more[:-5]
        more = (outs, stage, stage_sems)
        loads = []
        for i, (source, target) in enumerate(zip((own, ends), targets)):
            loads.append(pltpu.make_async_copy(source, target, window_sems.at[i]))
            loads[i].start()
        own, ends = targets
    slot, plan = 0, []
    for a, b in cells:
        found = terms(a, b)
        start, run, copies = slot, 0, []
        for i, (k, _, _) in enumerate(found):
            run += 1
            if i + 1 == len(found) or found[i + 1][0] != k + 1:
                source = blocks.at[a, b, pl.ds(k + 1 - run, run)]
                copies.append(pltpu.make_async_copy(source, held.at[pl.ds(slot, run)], sems.at[slot]))
                copies[-1].start()
                slot, run = slot + run, 0
        plan.append((start, copies, found))

    first = at[0] == 0
    for a in range(WIDE):
        near, far = pair[a, 0], present(at[3], outer[a, 0])
        sides[0, a] = jnp.where(first, far, near)
        sides[1, a] = jnp.where(first, near, far)
    if fetch:
        for load in loads:
            load.wait()

    def window(a, b):
        if b == 0:
            return sides[0, a]
        if b == WIDE - 1:
            return sides[1, a]
        if a in (0, WIDE - 1):
            return ends[0 if a == 0 else 1, b - 1]
        return own[a - 1, b - 1]

    line = held.shape[-1]
    for (a, b), (start, copies, found) in zip(cells, plan):
        for copy in copies:
            copy.wait()
        sources = jnp.concatenate([window(sa, sb) for _, sa, sb in found], axis=1)
        weights = held[start : start + len(found)].reshape(len(found) * line, line)
        put(a, b, jnp.dot(sources, weights, preferred_element_type=F32), at, more)
    if fetch:
        for i in range(2):
            for a in range(WIDE):
                pltpu.make_async_copy(stage.at[i, a], outs[i].at[a, 0], stage_sems.at[i, a]).wait()


def line_solve(cells, put, shapes, windows, line_inverse, extra=(), fetch=False):
    count = sum(len(terms(a, b)) for a, b in cells)
    line = line_inverse.shape[-1]
    rhs = windows[0].shape[2]

    def body(*refs):
        line_kernel(cells, put, fetch, *refs)

    out_specs, scratch = [VMEM] * len(shapes), []
    if fetch:
        shapes = shapes + [struct(w.shape, w.dtype) for w in windows[:2]]
        out_specs = [HBM] * 2 + [VMEM] * 2
        scratch = [
            pltpu.SemaphoreType.DMA((2,)),
            pltpu.VMEM((2, WIDE, rhs, line), BF16),
            pltpu.SemaphoreType.DMA((2, WIDE)),
        ]
    return pl.pallas_call(
        body,
        out_shape=shapes,
        in_specs=[ANY if fetch else VMEM] * 2 + [VMEM] * 2 + [HBM] + [VMEM] * len(extra),
        out_specs=out_specs,
        scratch_shapes=scratch
        + [
            pltpu.VMEM((2, WIDE, rhs, line), BF16),
            pltpu.VMEM((count, line, line), line_inverse.dtype),
            pltpu.SemaphoreType.DMA((count,)),
        ],
        compiler_params=limit(42),
        cost_estimate=estimate(2 * count * rhs * line * line, count * line * line * 2),
    )(*windows, line_inverse, *extra)


def put_rim(a, b, value, at, refs):
    outs, stage, sems = refs
    value = value.astype(BF16)
    first = at[0] == 0
    to_pair = first if b else jnp.logical_not(first)
    for i, chosen in ((0, to_pair), (1, jnp.logical_not(to_pair))):

        @pl.when(chosen)
        def _(i=i):
            stage[i, a] = value
            pltpu.make_async_copy(stage.at[i, a], outs[i].at[a, 0], sems.at[i, a]).start()


def returned(at, from_pair, from_outer, a, b):
    near, far = from_pair[a, 0], present(at[3], from_outer[a, 0])
    return jnp.where((at[0] == 0) == (b == 1), far, near).astype(F32)


def put_rows(a, b, value, at, refs):
    from_pair, from_outer, near, far = refs
    value = (value + returned(at, from_pair, from_outer, a, b)).astype(BF16)
    to_near = (at[4] == 0) == (a != 0)

    @pl.when(to_near)
    def _():
        near[0, b - 1] = value

    @pl.when(jnp.logical_not(to_near))
    def _():
        far[0, b - 1] = value


def put_inner(a, b, value, at, refs):
    refs[-1][a - 1, b - 1] = value


def columns(near, far, rounded):
    rhs, line = rounded.shape[2:]

    def body(near, far, rounded, pair, outer, own, ends):
        at = position()
        first, even = at[0] == 0, at[4] == 0
        for a in range(WIDE):
            if a in (0, WIDE - 1):
                for b in range(2):
                    low, high = (far, near) if a == 0 else (near, far)
                    ends[a // 2, b] = present(at[1 + a // 2], jnp.where(even, low[0, b], high[0, b]))
                left, right = ends[a // 2, 0], ends[a // 2, 1]
            else:
                left, right = rounded[a - 1, 0], rounded[a - 1, 1]
                own[a - 1, 0], own[a - 1, 1] = left, right
            pair[a, 0] = jnp.where(first, right, left)
            outer[a, 0] = jnp.where(first, left, right)

    out, square = struct((WIDE, 1, rhs, line), BF16), struct(rounded.shape, BF16)
    return pl.pallas_call(
        body,
        out_shape=[out, out, square, square],
        in_specs=[VMEM] * 3,
        out_specs=[VMEM] * 4,
        compiler_params=limit(4),
    )(near, far, rounded)


def rim_lines(windows, line_inverse):
    _, _, rhs, line = windows[0].shape
    column = struct((WIDE, 1, rhs, line), BF16)
    cells = [(a, b) for a in range(WIDE) for b in (0, WIDE - 1)]
    return line_solve(cells, put_rim, [column, column], windows, line_inverse, fetch=True)


def row_lines(windows, line_inverse, from_pair, from_outer):
    _, _, rhs, line = windows[0].shape
    row = struct((1, 2, rhs, line), BF16)
    cells = [(a, b) for a in (0, WIDE - 1) for b in (1, 2)]
    return line_solve(cells, put_rows, [row, row], windows, line_inverse, (from_pair, from_outer))


def inner_lines(windows, line_inverse):
    cells = [(a, b) for a in (1, 2) for b in (1, 2)]
    return line_solve(cells, put_inner, [struct(windows[0].shape, F32)], windows, line_inverse)[0]


def collect(inner, from_pair, from_outer, from_near, from_far):
    cx, cy, _, _ = inner.shape

    def body(inner, from_pair, from_outer, from_near, from_far, out):
        at = position()
        for a in range(cx):
            for b in range(cy):
                side = returned(at, from_pair, from_outer, a + 1, b + 1)
                low, high = (from_far, from_near) if a == 0 else (from_near, from_far)
                across = present(at[1 + a], jnp.where(at[4] == 0, low[0, b], high[0, b])).astype(F32)
                out[a, b] = inner[a, b] + side + across

    return pl.pallas_call(
        body,
        out_shape=struct(inner.shape, F32),
        in_specs=[VMEM] * 5,
        out_specs=VMEM,
        compiler_params=limit(8),
        cost_estimate=estimate(10**9, 4 * 10**6),
    )(inner, from_pair, from_outer, from_near, from_far)


def keep_mask(count, slots, rhs):
    return lax.broadcasted_iota(jnp.int32, (slots, rhs), 0) < count[0, 0]


def round_cells(residual_field):
    cx, cy, rhs, line = residual_field.shape

    def body(residual, rounded, near, far):
        even = position()[4] == 0
        for b in range(cy):
            first, second = residual[0, b].astype(BF16), residual[1, b].astype(BF16)
            rounded[0, b], rounded[1, b] = first, second
            near[0, b] = jnp.where(even, second, first)
            far[0, b] = jnp.where(even, first, second)

    row = struct((1, cy, rhs, line), BF16)
    return pl.pallas_call(
        body,
        out_shape=[struct(residual_field.shape, BF16), row, row],
        in_specs=[VMEM],
        out_specs=[VMEM] * 3,
        compiler_params=limit(4),
    )(residual_field)


def prepare(rounded, deflation, counts, factor, ring, blocks):
    slots, line = deflation.shape[2:]
    cx, cy, rhs, _ = rounded.shape
    width = factor.shape[1] // (ring * blocks)

    def body(count, rounded, vectors, factor, *refs):
        vector, parts = refs[0], refs[1 : 1 + ring]
        cut, sems = refs[1 + ring :]
        here = lax.axis_index("x")
        saves = []
        for step in range(ring):
            n = (step + 1) % ring
            there = lax.rem(here + n, ring)
            for j in range(blocks):
                start = pl.multiple_of((j * ring + there) * width, width)
                cut[n, j] = factor[:, pl.ds(start, width)].astype(BF16)
            saves.append(pltpu.make_async_copy(cut.at[n], parts[n], sems.at[n]))
            saves[-1].start()
        total = None
        for a in range(cx):
            for b in range(cy):
                part = lax.dot_general(
                    vectors[a, b], rounded[a, b], (((1,), (1,)), ((), ())), preferred_element_type=F32
                )
                total = part if total is None else total + part
        total = jnp.where(keep_mask(count, slots, rhs), total, 0.0).astype(BF16)
        vector[...] = total
        for save in saves:
            save.wait()

    return pl.pallas_call(
        body,
        out_shape=[struct((slots, rhs), BF16)] + [struct((blocks, slots, width), BF16)] * ring,
        in_specs=[SMEM, VMEM, VMEM, VMEM],
        out_specs=[VMEM] + [HBM] * ring,
        scratch_shapes=[
            pltpu.VMEM((ring, blocks, slots, width), BF16),
            pltpu.SemaphoreType.DMA((1 + ring,)),
        ],
        compiler_params=limit(6),
    )(counts, rounded, deflation, factor)


def spread_pair(mine, other, copies):
    slots, rhs = mine.shape

    def body(mine, other, out, made, sem):
        first = lax.axis_index("c") == 0
        low, high = jnp.where(first, mine[...], other[...]), jnp.where(first, other[...], mine[...])
        for i in range(copies):
            made[i, 0], made[i, 1] = low, high
        copy = pltpu.make_async_copy(made, out, sem)
        copy.start()
        copy.wait()

    shape = (copies, 2, slots, rhs)
    return pl.pallas_call(
        body,
        out_shape=struct(shape, BF16),
        in_specs=[VMEM, VMEM],
        out_specs=HBM,
        scratch_shapes=[pltpu.VMEM(shape, BF16), pltpu.SemaphoreType.DMA],
        compiler_params=limit(4),
    )(mine, other)


def halves(value):
    high = value.astype(BF16)
    return high, (value - high.astype(F32)).astype(BF16)


def lower(rows, gathered):
    sets = len(rows)
    blocks, slots, _ = rows[0].shape
    count, _, _, rhs = gathered.shape
    per = count // blocks

    def body(*refs):
        rows, (gathered, out) = refs[:sets], refs[sets:]
        total = None
        for j in range(blocks):
            pieces = []
            for y in range(per):
                pieces += [gathered[j * per + y, 0], gathered[j * per + y, 1]]
            factor = jnp.concatenate([r[j] for r in rows], 0)
            part = jnp.dot(factor, jnp.concatenate(pieces, 0), preferred_element_type=F32)
            total = part if total is None else total + part
        for n in range(sets):
            out[n] = total[n * slots : (n + 1) * slots]

    return pl.pallas_call(
        body,
        out_shape=struct((sets, slots, rhs), F32),
        in_specs=[VMEM] * (sets + 1),
        out_specs=VMEM,
        compiler_params=limit(8),
    )(*rows, gathered)


def raise_back(rows, partial, received):
    sets = len(rows)
    blocks, slots, width = rows[0].shape
    rhs = partial.shape[2]
    per = width // (2 * slots)

    def body(*refs):
        rows, partial, received = refs[:sets], refs[sets], refs[sets + 1 : 2 * sets]
        mine, other = refs[2 * sets :]
        first = lax.axis_index("c") == 0
        sums = []
        for n in range(sets):
            total = partial[n]
            for step in range(1, sets):
                total = total + received[step - 1][(n - step) % sets]
            sums.append(total)
        lowered_high, lowered_low = halves(jnp.concatenate(sums, 0))
        over = (((0,), (0,)), ((), ()))
        for j in range(blocks):
            factor = jnp.concatenate([r[j] for r in rows], 0)
            part = lax.dot_general(factor, lowered_high, over, preferred_element_type=F32)
            part = part + lax.dot_general(factor, lowered_low, over, preferred_element_type=F32)
            for y in range(per):
                a = part[2 * y * slots : (2 * y + 1) * slots]
                b = part[(2 * y + 1) * slots : (2 * y + 2) * slots]
                mine[j * per + y] = jnp.where(first, a, b)
                other[j * per + y] = jnp.where(first, b, a).astype(BF16)

    shape = (blocks * per, slots, rhs)
    return pl.pallas_call(
        body,
        out_shape=[struct(shape, F32), struct(shape, BF16)],
        in_specs=[VMEM] * (2 * sets),
        out_specs=[VMEM, VMEM],
        compiler_params=limit(8),
    )(*rows, partial, *received)


def leave(counts, first_level, terms_in, deflation):
    cx, cy, rhs, line = first_level.shape
    slots = deflation.shape[2]

    def body(count, first_level, terms_in, vectors, out, made, sems):
        total = terms_in[0].astype(F32)
        for i in range(1, terms_in.shape[0]):
            total = total + terms_in[i].astype(F32)
        solved = jnp.where(keep_mask(count, slots, rhs), total, 0.0).astype(BF16)
        saves = []
        for a in range(cx):
            for b in range(cy):
                value = lax.dot_general(
                    solved, vectors[a, b], (((0,), (0,)), ((), ())), preferred_element_type=F32
                )
                made[a, b] = value + first_level[a, b]
                saves.append(pltpu.make_async_copy(made.at[a, b], out.at[a, b], sems.at[a, b]))
                saves[-1].start()
        for save in saves:
            save.wait()

    return pl.pallas_call(
        body,
        out_shape=struct(first_level.shape, F32),
        in_specs=[SMEM, VMEM, VMEM, VMEM],
        out_specs=HBM,
        scratch_shapes=[pltpu.VMEM(first_level.shape, F32), pltpu.SemaphoreType.DMA((cx, cy))],
        compiler_params=limit(6),
    )(counts, first_level, terms_in, deflation)


def solution(mesh):
    n_grp, n_sub = mesh.shape["grp"], mesh.shape["sub"]
    sizes = {"zh": 2, "x": n_grp // 2, "zl": 2, "y": n_sub // 4, "c": 2}
    fine = Mesh(mesh.devices.reshape([sizes[a] for a in AXES]), AXES)

    def body(residual_field, line_inverse, deflation, counts, coarse_factor):
        tie = lax.optimization_barrier
        ring = sizes["x"]

        rounded, to_near, to_far = round_cells(residual_field)
        near, far = swap_pairs(to_near, GRP, n_grp, 0), swap_pairs(to_far, GRP, n_grp, 1)
        receivers = sizes["zh"] * sizes["zl"] * sizes["y"]
        vector, *parts = prepare(rounded, deflation, counts, coarse_factor, ring, sizes["zh"])
        moved = {n: rotate(parts[n], RING, ring, n) for n in (2, 1, 3)}
        rows = [parts[0]] + [moved[n] for n in range(1, ring)]
        spread = spread_pair(vector, swap(vector, "c"), receivers)
        far, spread, _ = tie((far, spread, parts[0]))
        to_pair, to_outer, own, ends = columns(near, far, rounded)
        outer, pair = swap_outward(to_outer, n_sub), swap(to_pair, "c")
        spread, _ = tie((spread, to_outer))
        gathered = lax.all_to_all(spread, SPREAD, 0, 0)
        outer, rows[0], rows[2], rows[1], rows[3] = tie((outer, rows[0], rows[2], rows[1], rows[3]))

        to_pair, to_outer, own, ends = rim_lines((own, ends, pair, outer), line_inverse)
        from_outer, from_pair = swap_outward(to_outer, n_sub), swap(to_pair, "c")
        gathered, _ = tie((gathered, to_outer))
        partial = lower(rows, gathered)
        moved = {n: rotate(partial, RING, ring, n) for n in (2, 1, 3)}
        received = [moved[n] for n in range(1, ring)]
        own, _ = tie((own, partial))
        to_near, to_far = row_lines((own, ends, pair, outer), line_inverse, from_pair, from_outer)
        partial, received[1], received[0], received[2], _ = tie((partial, received[1], received[0], received[2], to_near))
        own_terms, other_terms = raise_back(rows, partial, received)
        to_near, to_far, other_terms = tie((to_near, to_far, other_terms))
        from_near, from_far = swap_pairs(to_near, GRP, n_grp, 0), swap_pairs(to_far, GRP, n_grp, 1)
        terms_out = (own_terms + swap(other_terms, "c").astype(F32)).astype(BF16)
        terms_in = lax.all_to_all(terms_out, SPREAD, 0, 0)
        own, _ = tie((own, terms_out))
        inner = inner_lines((own, ends, pair, outer), line_inverse)
        inner, from_far = tie((inner, from_far))
        first_level = collect(inner, from_pair, from_outer, from_near, from_far)
        return leave(counts, first_level, terms_in, deflation)

    return jax.shard_map(
        body,
        mesh=fine,
        in_specs=(
            P(GRP, SUB, None, None),
            P(GRP, SUB, None, None, None),
            P(GRP, SUB, None, None),
            P(GRP, SUB),
            P(AXES, None),
        ),
        out_specs=P(GRP, SUB, None, None),
        check_vma=False,
    )
```
